256 devices in a mesh: lon: 16 (over z, x_hi), lat: 16 (over y, x_lo, core).
Axes of the slice: x: 4 (x_hi: 2, x_lo: 2; x = x_hi * 2 + x_lo), y: 4, z: 8, core: 2. Of those that a mesh axis runs over, the one named last changes fastest.
Arguments:
- temp: float32 [48, 256, 2048], P(None, 'lat', 'lon'), may hold values from -6 to 6
- salt: float32 [48, 256, 2048], P(None, 'lat', 'lon'), may hold values from -6 to 6
- east_speed: float32 [48, 256, 2048], P(None, 'lat', 'lon'), may hold values from -0.15 to 0.15
- north_speed: float32 [48, 256, 2048], P(None, 'lat', 'lon'), may hold values from -0.15 to 0.15
- mixing_h: float32 [48, 256, 2048], P(None, 'lat', 'lon'), may hold values from 0.01 to 0.08
- mixing_v: float32 [48, 256, 2048], P(None, 'lat', 'lon'), may hold values from 0.1 to 10
- wet: int32 [48, 256, 2048], P(None, 'lat', 'lon'), may hold values from 0 to 1, as said below
- bottom: int32 [256, 2048], P('lat', 'lon'), may hold values from 0 to 48, as said below
Outputs:
- temp_out: float32 [48, 256, 2048], P(None, 'lat', 'lon')
- salt_out: float32 [48, 256, 2048], P(None, 'lat', 'lon')
The draws below stay inside these ranges and needn't reach their ends.
Inputs may be any that keep to these rules, and one draw needn't show every extreme that they name: wet[k, y, x] is 1 exactly where k < bottom[y, x]. `bottom`: 0 marks land columns; every draw has land columns and columns 48 levels deep.
All inputs are finite; a program needn't handle non-finite values.
Results may differ from the reference program's by a relative error of at most 0.00002.
Values sent between devices are 32-bit elements; how exact they have to be, the bound alone decides.
No kernel may reach another device: no remote copies, remote signals or barrier semaphores. Data moves between devices by JAX's collectives and lax.ppermute only.
A program may use at most 128 MiB of HBM per device.

```python
import math
import jax
import jax.numpy as jnp
from jax import lax

NZ = 48
NY = 256
NX = 2048


def land_depth(key):
    coarse_key = jax.random.fold_in(key, 11)
    jitter_key = jax.random.fold_in(key, 12)
    coarse = jax.random.randint(coarse_key, ((NY + 15) // 16, (NX + 15) // 16), -(NZ // 2), NZ + NZ // 2 + 1)
    column_depth = jnp.repeat(jnp.repeat(coarse, 16, axis=0), 16, axis=1)[:NY, :NX]
    column_depth = column_depth + jax.random.randint(jitter_key, (NY, NX), -3, 4)
    column_depth = jnp.clip(column_depth, 0, NZ)
    column_depth = column_depth.at[NY // 2, 0].set(NZ)
    column_depth = column_depth.at[NY // 2, 1].set(0)
    return column_depth.astype(jnp.int32)


def draw_wet(key, part):
    column_depth = land_depth(key)
    levels = jnp.arange(NZ, dtype=jnp.int32).reshape(NZ, 1, 1)
    return (levels < column_depth[None]).astype(jnp.int32)


def draw_bottom(key, part):
    return land_depth(key)


def level_of(key, extent, pieces, low, top_value):
    gain, own = 1.0, jax.random.fold_in(key, 6)
    for dim, blocks in pieces:
        steps = jnp.exp(jax.random.uniform(jax.random.fold_in(own, dim), (blocks,), jnp.float32, low / len(pieces), top_value / len(pieces)))
        gain = gain * jnp.repeat(steps, extent[dim] // blocks).reshape([-1 if axis == dim else 1 for axis in range(len(extent))])
    return gain


def normal_values(stream_key, extent, deviation, reach, cuts=(), kind=jnp.bfloat16):
    result = deviation * jax.random.normal(stream_key, extent, jnp.float32)
    if cuts:
        result = result * level_of(stream_key, extent, cuts, -0.22, 0.18)
    return jnp.clip(result, -reach, reach).astype(kind)


def setup_inputs(seed: int = 0) -> dict:
    seeds = jax.random.split(jax.random.key(seed), 9)
    return {
        "temp": normal_values(seeds[0], (NZ, NY, NX), 1.0, 6.0, ((1, 16), (2, 16)), jnp.float32),
        "salt": normal_values(seeds[1], (NZ, NY, NX), 1.0, 6.0, ((1, 16), (2, 16)), jnp.float32),
        "east_speed": jnp.clip(jax.random.uniform(seeds[2], (NZ, NY, NX), jnp.float32, -0.15, 0.15) * level_of(seeds[2], (NZ, NY, NX), ((1, 16), (2, 16)), -0.4, 0.0), -0.15, 0.15),
        "north_speed": jnp.clip(jax.random.uniform(seeds[3], (NZ, NY, NX), jnp.float32, -0.15, 0.15) * level_of(seeds[3], (NZ, NY, NX), ((1, 16), (2, 16)), -0.4, 0.0), -0.15, 0.15),
        "mixing_h": jnp.clip(jnp.exp(math.log(0.08) - 2.0794415 * jax.random.uniform(seeds[4], (NZ, NY, NX), jnp.float32) ** level_of(seeds[4], (NZ, NY, NX), ((1, 16), (2, 16)), -0.2, 0.2)), 0.01, 0.08),
        "mixing_v": jnp.clip(jnp.exp(math.log(10.0) - 4.6051702 * jax.random.uniform(seeds[5], (NZ, NY, NX), jnp.float32) ** level_of(seeds[5], (NZ, NY, NX), ((1, 16), (2, 16)), -0.2, 0.2)), 0.1, 10.0),
        "wet": draw_wet(jax.random.fold_in(seeds[8], 71), 0),
        "bottom": draw_bottom(jax.random.fold_in(seeds[8], 71), 0),
    }


def face(left_side, right_side, velocity, diffuse, open_face):
    difference = right_side - left_side
    return open_face * (0.5 * velocity * (left_side + right_side) - 0.5 * jnp.abs(velocity) * difference - diffuse * difference)


def column_mix(lateral, coupling):
    coupling_above = jnp.concatenate([jnp.zeros_like(coupling[:1]), coupling[:-1]], 0)
    diagonal = 1.0 + coupling_above + coupling

    def downward(state, inputs):
        upper_prev, rhs_prev = state
        coupling_here, above_here, diagonal_here, rhs_here = inputs
        pivot_value = diagonal_here + above_here * upper_prev
        upper_next = -coupling_here / pivot_value
        rhs_next = (rhs_here + above_here[None] * rhs_prev) / pivot_value[None]
        return (upper_next, rhs_next), (upper_next, rhs_next)

    start_state = (jnp.zeros_like(coupling[0]), jnp.zeros_like(lateral[0]))
    unused_state, (uppers, rights) = lax.scan(downward, start_state, (coupling, coupling_above, diagonal, lateral))

    def upward(value_below, inputs):
        upper_here, rhs_here = inputs
        value_here = rhs_here - upper_here[None] * value_below
        return value_here, value_here

    unused_last, solved = lax.scan(upward, jnp.zeros_like(lateral[0]), (uppers, rights), reverse=True)
    return solved


def advance(tracers, east_speed, north_speed, mixing_h, wetness, coupling):
    east_flux = face(tracers[:, :, :, :-1], tracers[:, :, :, 1:], east_speed[:, None, :, :-1], mixing_h[:, None, :, :-1], (wetness[:, :, :-1] * wetness[:, :, 1:])[:, None])
    north_flux = face(tracers[:, :, :-1, :], tracers[:, :, 1:, :], north_speed[:, None, :-1, :], mixing_h[:, None, :-1, :], (wetness[:, :-1, :] * wetness[:, 1:, :])[:, None])
    lateral = tracers[:, :, 1:-1, 1:-1] - (east_flux[:, :, 1:-1, 1:] - east_flux[:, :, 1:-1, :-1]) - (north_flux[:, :, 1:, 1:-1] - north_flux[:, :, :-1, 1:-1])
    mixed = column_mix(lateral, coupling)
    return mixed * wetness[:, None, 1:-1, 1:-1]


def couple(mixing_v, bottom):
    levels = jnp.arange(mixing_v.shape[0]).astype(bottom.dtype).reshape(-1, 1, 1)
    return jnp.where(levels + 1 < bottom[None], mixing_v, 0.0)


def extend(field):
    widened = jnp.concatenate([field[:, :, -1:], field, field[:, :, :1]], 2)
    north_row = jnp.flip(widened[:, -1:, :], 2)
    south_row = jnp.zeros_like(widened[:, :1, :])
    return jnp.concatenate([south_row, widened, north_row], 1)


def reference(temp, salt, east_speed, north_speed, mixing_h, mixing_v, wet, bottom):
    wetness = wet.astype(jnp.float32)
    coupling = couple(mixing_v, bottom)
    wet_ext = extend(wetness)
    east_ext = extend(east_speed)
    north_ext = extend(north_speed)
    mixing_ext = extend(mixing_h)
    depth_levels, rows_all, columns_all = temp.shape
    tracers = jnp.stack([temp, salt], 1)
    for step_index in range(2):
        flattened = tracers.reshape(2 * depth_levels, rows_all, columns_all)
        extended = extend(flattened).reshape(depth_levels, 2, rows_all + 2, columns_all + 2)
        tracers = advance(extended, east_ext, north_ext, mixing_ext, wet_ext, coupling)
    return tracers[:, 0], tracers[:, 1]
```

```python
import functools

import jax
import jax.numpy as jnp
from jax import lax
from jax.experimental import pallas as pl
from jax.experimental.pallas import tpu as pltpu
from jax.sharding import PartitionSpec as P

F32 = jnp.float32
NF = 8


def lat_routes(count_lon, count_lat):
    first, second = [], []
    for i in range(count_lon):
        for j in range(count_lat):
            here = i * count_lat + j
            upward, downward = (first, second) if j % 2 else (second, first)
            if j == count_lat - 1:
                upward.append((here, (count_lon - 1 - i) * count_lat + j))
            else:
                upward.append((here, here + 1))
            if j > 0:
                downward.append((here, here - 1))
    return first, second


def lane_of(shape):
    return lax.broadcasted_iota(jnp.int32, shape, 1)


def row_of(shape):
    return lax.broadcasted_iota(jnp.int32, shape, 0)


def roll(x, shift, axis=1):
    size = x.shape[axis]
    if isinstance(shift, int):
        shift = shift % size
    return pltpu.roll(x, shift, axis)


def upwind(speed, mix):
    return jnp.maximum(speed, 0.0) + mix, jnp.minimum(speed, 0.0) - mix


def rows_kernel(NZ, NY, last, pos_ref, t_ref, s_ref, u_ref, v_ref, h_ref, m_ref, bot_ref, a_ref, b_ref):
    j = pos_ref[0]
    odd = lax.rem(j, 2) == 1
    lev = row_of((NZ, 128))
    lane = lane_of((NZ, 128))

    def message(row, inner, top):
        def at(ref, r):
            return ref[pl.ds(r, NZ, stride=NY), :]

        def sea(r):
            return (lev < bot_ref[r : r + 1, :]).astype(F32)

        w, w2 = sea(row), sea(inner)
        pe, qe = upwind(at(u_ref, row), at(h_ref, row))
        pe, qe = w * pe, w * qe
        east = jnp.where(lane < 127, roll(w, -1), 0.0)
        if top:
            pn, qn = upwind(at(v_ref, inner), at(h_ref, inner))
        else:
            pn, qn = upwind(at(v_ref, row), at(h_ref, row))
        both = w * w2
        cells, lats = [], []
        for ref in (t_ref, s_ref):
            c, c2 = w * at(ref, row), w2 * at(ref, inner)
            flux = east * (pe * c + qe * roll(c, -1))
            lat = c - flux + roll(flux, 1)
            if top:
                lat = lat + both * (pn * c2 + qn * c)
            else:
                lat = lat - both * (pn * c + qn * c2)
            cells.append(c)
            lats.append(lat)
        coupling = jnp.where(lev + 1 < bot_ref[row : row + 1, :], at(m_ref, row), 0.0)
        ends = jnp.where(lane == 127, pe, jnp.where(lane == 126, roll(qe, -1), 0.0))
        if top:
            po, qo = upwind(at(v_ref, row), at(h_ref, row))
            po, qo = w * po, w * qo
        else:
            po = qo = jnp.zeros_like(w)
        return cells + lats + [coupling, ends, po, qo]

    up = message(NY - 1, NY - 2, True)
    down = message(0, 1, False)
    for f in range(NF):
        a_ref[f * NZ : (f + 1) * NZ, :] = jnp.where(odd, up[f], down[f])
        b_ref[f * NZ : (f + 1) * NZ, :] = jnp.where(odd, down[f], up[f])
    bot_up = jnp.broadcast_to(bot_ref[NY - 1 : NY, :].astype(F32), (8, 128))
    bot_down = jnp.broadcast_to(bot_ref[0:1, :].astype(F32), (8, 128))
    a_ref[NF * NZ :, :] = jnp.where(odd, bot_up, bot_down)
    b_ref[NF * NZ :, :] = jnp.where(odd, bot_down, bot_up)

    @pl.when(j == last)
    def _():
        for r in range(0, NF * NZ + 8, 8):
            x = a_ref[r : r + 8, :]
            a_ref[r : r + 8, :] = jnp.take_along_axis(x, 127 - lane_of((8, 128)), axis=1)


def block_kernel(NZ, NY, t_ref, s_ref, u_ref, v_ref, h_ref, m_ref, bot_ref,
                 lt_ref, ls_ref, a0_ref, ae_ref, aw_ref, an_ref, as_ref, r_ref, g_ref, pk_ref):
    shape = (NY, 128)
    lane, row = lane_of(shape), row_of(shape)
    bot = bot_ref[...]
    east_in = lane < 127
    north_in = row < NY - 1

    def level(k, carry):
        above, g_above = carry[0], carry[1]
        packed = carry[2:]
        here = pl.ds(pl.multiple_of(k * NY, NY), NY)
        w = (k < bot).astype(F32)
        pe, qe = upwind(u_ref[here, :], h_ref[here, :])
        pn, qn = upwind(v_ref[here, :], h_ref[here, :])
        pe, qe = w * pe, w * qe
        we = jnp.where(east_in, roll(w, -1), 0.0)
        wn = w * jnp.where(north_in, roll(w, -1, 0), 0.0)
        pem, qem = pe * we, qe * we
        pnm, qnm = pn * wn, qn * wn
        cells, lats = [], []
        for src, dst in ((t_ref, lt_ref), (s_ref, ls_ref)):
            c = w * src[here, :]
            fe = pem * c + qem * roll(c, -1)
            fn = pnm * c + qnm * roll(c, -1, 0)
            lat = c - (fe - roll(fe, 1)) - (fn - roll(fn, 1, 0))
            dst[here, :] = lat
            cells.append(c)
            lats.append(lat)
        a0_ref[here, :] = 1.0 - pem - pnm + roll(qem, 1) + roll(qnm, 1, 0)
        ae_ref[here, :] = -qem
        aw_ref[here, :] = roll(pem, 1)
        an_ref[here, :] = -qnm
        as_ref[here, :] = roll(pnm, 1, 0)
        b = jnp.where(k + 1 < bot, m_ref[here, :], 0.0)
        r = 1.0 / (1.0 + above + b - above * g_above)
        g = b * r
        r_ref[here, :] = r
        g_ref[here, :] = g
        mine = lax.shift_right_logical(lane, 1) == k
        fields = cells + lats + [r, g, pe, qe]
        packed = tuple(jnp.where(mine, roll(x, 2 * k + 1), p) for x, p in zip(fields, packed))
        return (b, g) + packed

    zero = jnp.zeros(shape, F32)
    out = lax.fori_loop(0, NZ, level, (zero,) * 10)
    for f in range(8):
        pk_ref[f * NY : (f + 1) * NY, :] = out[2 + f]


def rim_rows(NZ, NY, last, pos_ref, ra_ref, rb_ref, t_ref, s_ref, v_ref, h_ref, bot_ref):
    j = pos_ref[0]
    odd = lax.rem(j, 2) == 1
    normal = (j != last).astype(F32)
    lev = row_of((NZ, 128))

    def south(f):
        return jnp.where(odd, rb_ref[f * NZ : (f + 1) * NZ, :], ra_ref[f * NZ : (f + 1) * NZ, :])

    def north(f):
        return jnp.where(odd, ra_ref[f * NZ : (f + 1) * NZ, :], rb_ref[f * NZ : (f + 1) * NZ, :])

    bots = jnp.where(odd, rb_ref[NF * NZ :, :], ra_ref[NF * NZ :, :])
    botn = jnp.where(odd, ra_ref[NF * NZ :, :], rb_ref[NF * NZ :, :])
    levf = lev.astype(F32)
    ws = (levf < bots[0:1, :]).astype(F32)
    wn = (levf < botn[0:1, :]).astype(F32)
    w0 = (lev < bot_ref[0:1, :]).astype(F32)
    w15 = (lev < bot_ref[NY - 1 : NY, :]).astype(F32)
    top = pl.ds(NY - 1, NZ, stride=NY)
    low = pl.ds(0, NZ, stride=NY)
    p15, q15 = upwind(v_ref[top, :], h_ref[top, :])
    p15, q15 = w15 * wn * p15, w15 * wn * q15
    als, bes = w0 * south(6), w0 * south(7)
    pf, qf = w15 * north(6), w15 * north(7)
    res = dict(bots=bots, botn=botn, als=als, bes=bes, p15=p15, q15=q15, south=south, north=north)
    fs, fn, gn = [], [], []
    for n, ref in enumerate((t_ref, s_ref)):
        c0, c15 = w0 * ref[low, :], w15 * ref[top, :]
        cs, cn = south(n), north(n)
        fs.append(als * cs + bes * c0)
        own = p15 * c15 + q15 * cn
        fn.append(own)
        gn.append(normal * own - (pf * cn + qf * c15))
    res.update(fs=fs, fn=fn, gn=gn)
    return res


def columns_kernel(NZ, NY, last, pos_ref, ra_ref, rb_ref, t_ref, s_ref, v_ref, h_ref, bot_ref, pk_ref, out_ref):
    x = rim_rows(NZ, NY, last, pos_ref, ra_ref, rb_ref, t_ref, s_ref, v_ref, h_ref, bot_ref)
    lev, lane = row_of((NZ, 128)), lane_of((NZ, 128))
    is_east, is_west = lane == 2 * lev, lane == 2 * lev + 1

    def diagonal(e, w):
        e = jnp.broadcast_to(e, (NZ, 128))
        w = jnp.broadcast_to(w, (NZ, 128))
        return jnp.sum(jnp.where(is_east, e, jnp.where(is_west, w, 0.0)), axis=0, keepdims=True)

    def ends(v):
        return diagonal(v[:, 127:128], v[:, 0:1])

    south, north = x["south"], x["north"]
    out_ref[0 : 8 * NY, :] = pk_ref[...]
    for n in range(2):
        base = (2 + n) * NY
        out_ref[base : base + 1, :] += ends(x["fs"][n])
        out_ref[base + NY - 1 : base + NY, :] -= ends(x["fn"][n])
    c = 8 * NY
    out_ref[c : c + 24, :] = jnp.zeros((24, 128), F32)
    for n in range(2):
        out_ref[c + 2 * n : c + 2 * n + 1, :] = ends(south(n))
        out_ref[c + 2 * n + 1 : c + 2 * n + 2, :] = ends(north(n))
    es, en = south(5), north(5)
    for r, e in enumerate((es, en)):
        pv = diagonal(e[:, 127:128], e[:, 0:1])
        qv = diagonal(e[:, 126:127], e[:, 1:2])
        for n in range(2):
            out_ref[c + 8 + 2 * n + r : c + 9 + 2 * n + r, :] = pv
            out_ref[c + 16 + 2 * n + r : c + 17 + 2 * n + r, :] = qv
    out_ref[c + 24 : c + 24 + NY, :] = bot_ref[...].astype(F32)
    side = row_of((8, 128))
    out_ref[c + 24 + NY : c + 32 + NY, :] = jnp.where(lax.rem(side, 2) == 0, x["bots"], x["botn"])


def ghost_rows_kernel(NZ, NY, last, pos_ref, ra_ref, rb_ref, t_ref, s_ref, v_ref, h_ref, bot_ref,
                      lt_in, ls_in, a0_in, an_in, as_in,
                      lt_ref, ls_ref, a0_ref, an_ref, as_ref, gl_ref, gr_ref, gg_ref, b_scr):
    x = rim_rows(NZ, NY, last, pos_ref, ra_ref, rb_ref, t_ref, s_ref, v_ref, h_ref, bot_ref)
    south, north = x["south"], x["north"]
    top = pl.ds(NY - 1, NZ, stride=NY)
    low = pl.ds(0, NZ, stride=NY)
    for src, dst in ((lt_in, lt_ref), (ls_in, ls_ref), (a0_in, a0_ref), (an_in, an_ref), (as_in, as_ref)):
        dst[...] = src[...]
    for n, (src, dst) in enumerate(((lt_in, lt_ref), (ls_in, ls_ref))):
        dst[low, :] = src[low, :] + x["fs"][n]
        dst[top, :] = src[top, :] - x["fn"][n]
    a0_ref[low, :] = a0_in[low, :] + x["bes"]
    a0_ref[top, :] = a0_in[top, :] - x["p15"]
    as_ref[low, :] = x["als"]
    an_ref[top, :] = -x["q15"]
    for n in range(2):
        gl_ref[pl.ds(2 * n, NZ, stride=8), :] = south(2 + n) - x["fs"][n]
        gl_ref[pl.ds(2 * n + 1, NZ, stride=8), :] = north(2 + n) + x["gn"][n]
        b_scr[pl.ds(2 * n, NZ, stride=8), :] = south(4)
        b_scr[pl.ds(2 * n + 1, NZ, stride=8), :] = north(4)
    zero = jnp.zeros((NZ, 128), F32)
    for n in range(4, 8):
        gl_ref[pl.ds(n, NZ, stride=8), :] = zero
        b_scr[pl.ds(n, NZ, stride=8), :] = zero

    def level(k, carry):
        above, g_above = carry
        here = pl.ds(pl.multiple_of(k * 8, 8), 8)
        b = b_scr[here, :]
        r = 1.0 / (1.0 + above + b - above * g_above)
        g = b * r
        gr_ref[here, :] = r
        gg_ref[here, :] = g
        return b, g

    z8 = jnp.zeros((8, 128), F32)
    lax.fori_loop(0, NZ, level, (z8, z8))


def steps_kernel(NZ, NY, rw_ref, re_ref, own_ref, lt_ref, ls_ref, a0_ref, ae_ref, aw_ref, an_ref, as_ref,
                 r_ref, g_ref, gl_ref, gr_ref, gg_ref, bot_ref, to_ref, so_ref,
                 yt, ys, ct, cs, yte, yse, re_s, ge_s, yr):
    shape = (NY, 128)
    PAD = NY + 16
    lane = lane_of(shape)
    lane8 = lane_of((8, 128))
    edge = (lane == 0) | (lane == 127)
    edge8 = (lane8 == 0) | (lane8 == 127)
    even, even8 = lax.rem(lane, 2) == 0, lax.rem(lane8, 2) == 0
    klane = lax.shift_right_logical(lane, 1).astype(F32)
    klane8 = lax.shift_right_logical(lane8, 1).astype(F32)

    def own(base, size):
        return own_ref[base : base + size, :]

    def ghost(base, size):
        ev = even if size == NY else even8
        return jnp.where(ev, roll(re_ref[base : base + size, :], -1), roll(rw_ref[base : base + size, :], 1))

    cb = 8 * NY
    bb = cb + 24

    def bottoms(base, size):
        ev = even if size == NY else even8
        sh = (size, 128)
        o, w, e = own(base, size), rw_ref[base : base + size, :], re_ref[base : base + size, :]

        def spread(x, col):
            return jnp.broadcast_to(x[:, col : col + 1], sh)

        mine = jnp.where(ev, spread(o, 127), spread(o, 0))
        theirs = jnp.where(ev, spread(e, 0), spread(w, 127))
        return mine, theirs

    bo, bg = bottoms(bb, NY)
    wo, wg = (klane < bo).astype(F32), (klane < bg).astype(F32)
    bot_edge = jnp.where(lane == 127, bg[:, 0:1], bg[:, 1:2])
    po = jnp.where(even, own(6 * NY, NY), 0.0)
    qo = jnp.where(even, own(7 * NY, NY), 0.0)
    pg = jnp.where(even, 0.0, ghost(6 * NY, NY))
    qg = jnp.where(even, 0.0, ghost(7 * NY, NY))
    alpha = wo * pg - wg * qo
    beta = wo * qg - wg * po
    corr = [alpha * ghost(n * NY, NY) + beta * own(n * NY, NY) for n in range(2)]
    glat = [ghost((2 + n) * NY, NY) - corr[n] for n in range(2)]
    gr, gg = ghost(4 * NY, NY), ghost(5 * NY, NY)

    bo8, bg8 = bottoms(bb + NY, 8)
    wo8, wg8 = (klane8 < bo8).astype(F32), (klane8 < bg8).astype(F32)
    co, cg = own(cb, 8), ghost(cb, 8)
    corner = wo8 * (ghost(cb + 8, 8) * cg + ghost(cb + 16, 8) * co) - wg8 * (own(cb + 8, 8) * co + own(cb + 16, 8) * cg)
    bot_rows = own(bb + NY, 8)
    bot = bot_ref[...]

    def down1(k, carry):
        gp, y0, y1, gep, e0, e1, ggp, yrow = carry
        here = pl.ds(pl.multiple_of(k * NY, NY), NY)
        here8 = pl.ds(pl.multiple_of(k * 8, 8), 8)
        turn = 127 - 2 * k
        y0 = lt_ref[here, :] + jnp.where(edge, roll(corr[0], turn), 0.0) + gp * y0
        y1 = ls_ref[here, :] + jnp.where(edge, roll(corr[1], turn), 0.0) + gp * y1
        e0 = roll(glat[0], turn) + gep * e0
        e1 = roll(glat[1], turn) + gep * e1
        yrow = gl_ref[here8, :] + jnp.where(edge8, roll(corner, turn), 0.0) + ggp * yrow
        yt[here, :] = y0
        ys[here, :] = y1
        yte[here, :] = e0
        yse[here, :] = e1
        yr[here8, :] = yrow
        ge = roll(gg, turn)
        re_s[here, :] = roll(gr, turn)
        ge_s[here, :] = ge
        return g_ref[here, :], y0, y1, ge, e0, e1, gg_ref[here8, :], yrow

    z, z8 = jnp.zeros(shape, F32), jnp.zeros((8, 128), F32)
    lax.fori_loop(0, NZ, down1, (z, z, z, z, z, z, z8, z8))

    def up1(n, carry):
        x0, x1, e0, e1, xr = carry
        k = NZ - 1 - n
        here = pl.ds(pl.multiple_of(k * NY, NY), NY)
        here8 = pl.ds(pl.multiple_of(k * 8, 8), 8)
        r, g = r_ref[here, :], g_ref[here, :]
        x0 = r * yt[here, :] + g * x0
        x1 = r * ys[here, :] + g * x1
        w = k < bot
        inner = pl.ds(pl.multiple_of(k * PAD + 8, 8), NY)
        ct[inner, :] = jnp.where(w, x0, 0.0)
        cs[inner, :] = jnp.where(w, x1, 0.0)
        r, g = re_s[here, :], ge_s[here, :]
        e0 = r * yte[here, :] + g * e0
        e1 = r * yse[here, :] + g * e1
        kf = k.astype(F32)
        we = kf < bot_edge
        yte[here, :] = jnp.where(we, e0, 0.0)
        yse[here, :] = jnp.where(we, e1, 0.0)
        xr = gr_ref[here8, :] * yr[here8, :] + gg_ref[here8, :] * xr
        c = jnp.where(kf < bot_rows, xr, 0.0)
        ct[pl.ds(k * PAD + 7, 1), :] = c[0:1, :]
        ct[pl.ds(k * PAD + 8 + NY, 1), :] = c[1:2, :]
        cs[pl.ds(k * PAD + 7, 1), :] = c[2:3, :]
        cs[pl.ds(k * PAD + 8 + NY, 1), :] = c[3:4, :]
        return x0, x1, e0, e1, xr

    lax.fori_loop(0, NZ, up1, (z, z, z, z, z8))

    def down2(k, carry):
        gp, y0, y1 = carry
        here = pl.ds(pl.multiple_of(k * NY, NY), NY)
        turn = 127 - 2 * k
        al = roll(alpha, turn)
        a0 = a0_ref[here, :] + jnp.where(edge, roll(beta, turn), 0.0)
        ae = jnp.where(lane == 127, al, ae_ref[here, :])
        aw = jnp.where(lane == 0, al, aw_ref[here, :])
        an, as_ = an_ref[here, :], as_ref[here, :]

        def lateral(c_ref, e_ref):
            c = c_ref[pl.ds(k * PAD + 8, NY), :]
            rim = e_ref[here, :]
            east = jnp.where(lane == 127, rim, roll(c, -1))
            west = jnp.where(lane == 0, rim, roll(c, 1))
            return (
                a0 * c + ae * east + aw * west
                + an * c_ref[pl.ds(k * PAD + 9, NY), :] + as_ * c_ref[pl.ds(k * PAD + 7, NY), :]
            )

        y0 = lateral(ct, yte) + gp * y0
        y1 = lateral(cs, yse) + gp * y1
        yt[here, :] = y0
        ys[here, :] = y1
        return g_ref[here, :], y0, y1

    lax.fori_loop(0, NZ, down2, (z, z, z))

    def up2(n, carry):
        x0, x1 = carry
        k = NZ - 1 - n
        here = pl.ds(pl.multiple_of(k * NY, NY), NY)
        r, g = r_ref[here, :], g_ref[here, :]
        x0 = r * yt[here, :] + g * x0
        x1 = r * ys[here, :] + g * x1
        w = k < bot
        to_ref[here, :] = jnp.where(w, x0, 0.0)
        so_ref[here, :] = jnp.where(w, x1, 0.0)
        return x0, x1

    lax.fori_loop(0, NZ, up2, (z, z))


VM = pl.BlockSpec(memory_space=pltpu.VMEM)
SM = pl.BlockSpec(memory_space=pltpu.SMEM)


def vmem(*shape):
    return pltpu.VMEM(shape, F32)


def call(kernel, n_in, outs, scratch=(), smem=False, cost=0, keep=True):
    specs = [SM] * smem + [VM] * (n_in - smem)
    shapes = [pltpu.VMEM(o, F32) if keep else jax.ShapeDtypeStruct(o, F32) for o in outs]
    return pl.pallas_call(
        kernel,
        out_shape=shapes,
        in_specs=specs,
        out_specs=[VM] * len(outs),
        scratch_shapes=list(scratch),
        compiler_params=pltpu.CompilerParams(vmem_limit_bytes=40 << 20),
        cost_estimate=pl.CostEstimate(flops=cost, bytes_accessed=cost, transcendentals=0) if cost else None,
    )


def per_device(temp, salt, east_speed, north_speed, mixing_h, mixing_v, wet, bottom):
    NZ, NY, NX = temp.shape
    count_lat, count_lon = lax.axis_size("lat"), lax.axis_size("lon")
    last = count_lat - 1
    flat = (NZ * NY, NX)
    t, s, u, v, h, m = (a.reshape(flat) for a in (temp, salt, east_speed, north_speed, mixing_h, mixing_v))
    pos = lax.axis_index("lat").astype(jnp.int32).reshape(1)
    rows_msg = (NF * NZ + 8, NX)
    first, second = lat_routes(count_lon, count_lat)
    axes = ("lon", "lat")

    msg_a, msg_b = call(functools.partial(rows_kernel, NZ, NY, last), 8, [rows_msg] * 2, smem=True)(
        pos, t, s, u, v, h, m, bottom
    )
    ra = lax.ppermute(msg_a, axes, first)
    rb = lax.ppermute(msg_b, axes, second)
    lt, ls, a0, ae, aw, an, as_, r, g, pk = call(
        functools.partial(block_kernel, NZ, NY), 7, [flat] * 9 + [(8 * NY, NX)], cost=10_000_000
    )(t, s, u, v, h, m, bottom)
    cols_msg = (8 * NY + 24 + NY + 8, NX)
    (cols,) = call(functools.partial(columns_kernel, NZ, NY, last), 9, [cols_msg], smem=True)(
        pos, ra, rb, t, s, v, h, bottom, pk
    )
    from_west = lax.ppermute(cols, "lon", [(i, (i + 1) % count_lon) for i in range(count_lon)])
    from_east = lax.ppermute(cols, "lon", [((i + 1) % count_lon, i) for i in range(count_lon)])
    ghost = (NZ * 8, NX)
    lt, ls, a0, an, as_, gl, gr, gg = call(
        functools.partial(ghost_rows_kernel, NZ, NY, last), 13, [flat] * 5 + [ghost] * 3,
        scratch=[vmem(*ghost)], smem=True, cost=10_000_000,
    )(pos, ra, rb, t, s, v, h, bottom, lt, ls, a0, an, as_)
    pad = (NZ * (NY + 16), NX)
    out = call(
        functools.partial(steps_kernel, NZ, NY), 16, [flat] * 2,
        scratch=[vmem(*flat), vmem(*flat), vmem(*pad), vmem(*pad)] + [vmem(*flat)] * 4 + [vmem(*ghost)], keep=False,
    )(from_west, from_east, cols, lt, ls, a0, ae, aw, an, as_, r, g, gl, gr, gg, bottom)
    return tuple(o.reshape(temp.shape) for o in out)


def solution(mesh):
    field = P(None, "lat", "lon")
    return jax.shard_map(
        per_device,
        mesh=mesh,
        in_specs=(field,) * 7 + (P("lat", "lon"),),
        out_specs=(field, field),
        check_vma=False,
    )
```

```python
import functools

import jax
import jax.numpy as jnp
from jax import lax
from jax.experimental import pallas as pl
from jax.experimental.pallas import tpu as pltpu
from jax.sharding import PartitionSpec as P

F32 = jnp.float32
NF = 8


def lat_routes(count_lon, count_lat):
    first, second = [], []
    for i in range(count_lon):
        for j in range(count_lat):
            here = i * count_lat + j
            upward, downward = (first, second) if j % 2 else (second, first)
            if j == count_lat - 1:
                upward.append((here, (count_lon - 1 - i) * count_lat + j))
            else:
                upward.append((here, here + 1))
            if j > 0:
                downward.append((here, here - 1))
    return first, second


def lane_of(shape):
    return lax.broadcasted_iota(jnp.int32, shape, 1)


def row_of(shape):
    return lax.broadcasted_iota(jnp.int32, shape, 0)


def roll(x, shift, axis=1):
    size = x.shape[axis]
    if isinstance(shift, int):
        shift = shift % size
    return pltpu.roll(x, shift, axis)


def in_turn(jobs, apart):
    running, waiting, step = [], list(jobs), 0
    while running or waiting:
        if waiting and step % apart == 0:
            running.append(waiting.pop(0))
        running = [job for job in running if next(job, "end") != "end"]
        step += 1


def upwind(speed, mix):
    return jnp.maximum(speed, 0.0) + mix, jnp.minimum(speed, 0.0) - mix


def rows_kernel(NZ, NY, last, pos_ref, *refs):
    sources, (a_ref, b_ref), kept, sems = refs[:7], refs[7:9], refs[9:16], refs[16]
    t_ref, s_ref, u_ref, v_ref, h_ref, m_ref, bot_ref = kept
    size = NZ * NY
    copies = []
    for n in (6, 0, 1, 2, 4, 3, 5):
        there = kept[n] if n == 6 else kept[n].at[pl.ds(0, size)]
        copies.append(pltpu.make_async_copy(sources[n], there, sems.at[n]))
        copies[-1].start()
    for n in range(6):
        kept[n][size:, :] = jnp.zeros((8, 128), F32)
    for copy in copies:
        copy.wait()
    j = pos_ref[0]
    odd = lax.rem(j, 2) == 1
    lev = row_of((NZ, 128))
    lane = lane_of((NZ, 128))

    def message(row, inner, top):
        def at(ref, r):
            return ref[pl.ds(r, NZ, stride=NY), :]

        def sea(r):
            return (lev < bot_ref[r : r + 1, :]).astype(F32)

        w, w2 = sea(row), sea(inner)
        pe, qe = upwind(at(u_ref, row), at(h_ref, row))
        pe, qe = w * pe, w * qe
        east = jnp.where(lane < 127, roll(w, -1), 0.0)
        if top:
            pn, qn = upwind(at(v_ref, inner), at(h_ref, inner))
        else:
            pn, qn = upwind(at(v_ref, row), at(h_ref, row))
        both = w * w2
        cells, lats = [], []
        for ref in (t_ref, s_ref):
            c, c2 = w * at(ref, row), w2 * at(ref, inner)
            flux = east * (pe * c + qe * roll(c, -1))
            lat = c - flux + roll(flux, 1)
            if top:
                lat = lat + both * (pn * c2 + qn * c)
            else:
                lat = lat - both * (pn * c + qn * c2)
            cells.append(c)
            lats.append(lat)
        coupling = jnp.where(lev + 1 < bot_ref[row : row + 1, :], at(m_ref, row), 0.0)
        ends = jnp.where(lane == 127, pe, jnp.where(lane == 126, roll(qe, -1), 0.0))
        if top:
            po, qo = upwind(at(v_ref, row), at(h_ref, row))
            po, qo = w * po, w * qo
        else:
            po = qo = jnp.zeros_like(w)
        return cells + lats + [coupling, ends, po, qo]

    up = message(NY - 1, NY - 2, True)
    down = message(0, 1, False)
    for f in range(NF):
        a_ref[f * NZ : (f + 1) * NZ, :] = jnp.where(odd, up[f], down[f])
        b_ref[f * NZ : (f + 1) * NZ, :] = jnp.where(odd, down[f], up[f])
    bot_up = jnp.broadcast_to(bot_ref[NY - 1 : NY, :].astype(F32), (8, 128))
    bot_down = jnp.broadcast_to(bot_ref[0:1, :].astype(F32), (8, 128))
    a_ref[NF * NZ :, :] = jnp.where(odd, bot_up, bot_down)
    b_ref[NF * NZ :, :] = jnp.where(odd, bot_down, bot_up)

    @pl.when(j == last)
    def _():
        for r in range(0, NF * NZ + 8, 8):
            x = a_ref[r : r + 8, :]
            a_ref[r : r + 8, :] = jnp.take_along_axis(x, 127 - lane_of((8, 128)), axis=1)


def block_kernel(NZ, NY, t_ref, s_ref, u_ref, v_ref, h_ref, m_ref, bot_ref,
                 lt_ref, ls_ref, pe_ref, qe_ref, pn_ref, qn_ref, r_ref, g_ref, pk_ref):
    shape = (NY, 128)
    lane, row = lane_of(shape), row_of(shape)
    bot = bot_ref[...]
    bot_e = jnp.where(lane < 127, roll(bot, -1), 0)
    bot_n = jnp.where(row < NY - 1, roll(bot, -1, 0), 0)
    pair = lax.shift_right_logical(lane, 1)
    zero = jnp.zeros(shape, F32)
    pn_ref[0:8, :] = jnp.zeros((8, 128), F32)
    qn_ref[0:8, :] = jnp.zeros((8, 128), F32)
    packed = [zero] * 8
    chain = [zero, zero]

    def level(k):
        here = pl.ds(k * NY, NY)
        next_row = pl.ds(k * NY + 1, NY)
        sea, sea_e, sea_n = k < bot, k < bot_e, k < bot_n
        cells = [jnp.where(sea, src[here, :], 0.0) for src in (t_ref, s_ref)]
        easts = [roll(c, -1) for c in cells]
        yield
        yield
        yield
        yield
        yield
        h = h_ref[here, :]
        pe, qe = upwind(u_ref[here, :], h)
        pn, qn = upwind(v_ref[here, :], h)
        pe, qe = jnp.where(sea, pe, 0.0), jnp.where(sea, qe, 0.0)
        both_n = sea & sea_n
        pem, qem = jnp.where(sea_e, pe, 0.0), jnp.where(sea_e, qe, 0.0)
        pnm, qnm = jnp.where(both_n, pn, 0.0), jnp.where(both_n, qn, 0.0)
        pe_ref[here, :] = pem
        qe_ref[here, :] = qem
        pn_ref[pl.ds(k * NY + 8, NY), :] = pnm
        qn_ref[pl.ds(k * NY + 8, NY), :] = qnm
        parts, wests, souths = [], [], []
        for src, c, ce in zip((t_ref, s_ref), cells, easts):
            cn = jnp.where(sea_n, src[next_row, :], 0.0)
            fe = pem * c + qem * ce
            fn = pnm * c + qnm * cn
            parts.append(c - fe - fn)
            wests.append(roll(fe, 1))
            souths.append(roll(fn, 1, 0))
        b = jnp.where(k + 1 < bot, m_ref[here, :], 0.0)
        above, g = chain
        r = 1.0 / (1.0 + above + b - above * g)
        g = b * r
        chain[:] = b, g
        r_ref[here, :] = r
        g_ref[here, :] = g
        first = [roll(x, 2 * k + 1) for x in cells + [r, g, pe, qe]]
        yield
        yield
        yield
        yield
        yield
        lats = [x + y + z for x, y, z in zip(parts, wests, souths)]
        lt_ref[here, :] = lats[0]
        ls_ref[here, :] = lats[1]
        moved = first[:2] + [roll(x, 2 * k + 1) for x in lats] + first[2:]
        yield
        yield
        yield
        yield
        yield
        mine = pair == k
        packed[:] = [jnp.where(mine, x, p) for x, p in zip(moved, packed)]

    in_turn([level(k) for k in range(NZ)], 1)
    for f in range(8):
        pk_ref[f * NY : (f + 1) * NY, :] = packed[f]


def rim_rows(NZ, NY, last, pos_ref, ra_ref, rb_ref, t_ref, s_ref, v_ref, h_ref, bot_ref):
    j = pos_ref[0]
    odd = lax.rem(j, 2) == 1
    normal = (j != last).astype(F32)
    lev = row_of((NZ, 128))

    def south(f):
        return jnp.where(odd, rb_ref[f * NZ : (f + 1) * NZ, :], ra_ref[f * NZ : (f + 1) * NZ, :])

    def north(f):
        return jnp.where(odd, ra_ref[f * NZ : (f + 1) * NZ, :], rb_ref[f * NZ : (f + 1) * NZ, :])

    bots = jnp.where(odd, rb_ref[NF * NZ :, :], ra_ref[NF * NZ :, :])
    botn = jnp.where(odd, ra_ref[NF * NZ :, :], rb_ref[NF * NZ :, :])
    levf = lev.astype(F32)
    ws = (levf < bots[0:1, :]).astype(F32)
    wn = (levf < botn[0:1, :]).astype(F32)
    w0 = (lev < bot_ref[0:1, :]).astype(F32)
    w15 = (lev < bot_ref[NY - 1 : NY, :]).astype(F32)
    top = pl.ds(NY - 1, NZ, stride=NY)
    low = pl.ds(0, NZ, stride=NY)
    p15, q15 = upwind(v_ref[top, :], h_ref[top, :])
    p15, q15 = w15 * wn * p15, w15 * wn * q15
    als, bes = w0 * south(6), w0 * south(7)
    pf, qf = w15 * north(6), w15 * north(7)
    res = dict(bots=bots, botn=botn, als=als, bes=bes, p15=p15, q15=q15, south=south, north=north)
    fs, fn, gn = [], [], []
    for n, ref in enumerate((t_ref, s_ref)):
        c0, c15 = w0 * ref[low, :], w15 * ref[top, :]
        cs, cn = south(n), north(n)
        fs.append(als * cs + bes * c0)
        own = p15 * c15 + q15 * cn
        fn.append(own)
        gn.append(normal * own - (pf * cn + qf * c15))
    res.update(fs=fs, fn=fn, gn=gn)
    return res


def columns_kernel(NZ, NY, last, pos_ref, ra_ref, rb_ref, t_ref, s_ref, v_ref, h_ref, bot_ref, pk_ref, out_ref):
    x = rim_rows(NZ, NY, last, pos_ref, ra_ref, rb_ref, t_ref, s_ref, v_ref, h_ref, bot_ref)
    lev, lane = row_of((NZ, 128)), lane_of((NZ, 128))
    is_east, is_west = lane == 2 * lev, lane == 2 * lev + 1

    def diagonal(e, w):
        e = jnp.broadcast_to(e, (NZ, 128))
        w = jnp.broadcast_to(w, (NZ, 128))
        return jnp.sum(jnp.where(is_east, e, jnp.where(is_west, w, 0.0)), axis=0, keepdims=True)

    def ends(v):
        return diagonal(v[:, 127:128], v[:, 0:1])

    south, north = x["south"], x["north"]
    out_ref[0 : 8 * NY, :] = pk_ref[...]
    for n in range(2):
        base = (2 + n) * NY
        out_ref[base : base + 1, :] += ends(x["fs"][n])
        out_ref[base + NY - 1 : base + NY, :] -= ends(x["fn"][n])
    c = 8 * NY
    out_ref[c : c + 24, :] = jnp.zeros((24, 128), F32)
    for n in range(2):
        out_ref[c + 2 * n : c + 2 * n + 1, :] = ends(south(n))
        out_ref[c + 2 * n + 1 : c + 2 * n + 2, :] = ends(north(n))
    es, en = south(5), north(5)
    for r, e in enumerate((es, en)):
        pv = diagonal(e[:, 127:128], e[:, 0:1])
        qv = diagonal(e[:, 126:127], e[:, 1:2])
        for n in range(2):
            out_ref[c + 8 + 2 * n + r : c + 9 + 2 * n + r, :] = pv
            out_ref[c + 16 + 2 * n + r : c + 17 + 2 * n + r, :] = qv
    out_ref[c + 24 : c + 24 + NY, :] = bot_ref[...].astype(F32)
    side = row_of((8, 128))
    out_ref[c + 24 + NY : c + 32 + NY, :] = jnp.where(lax.rem(side, 2) == 0, x["bots"], x["botn"])


def ghost_rows_kernel(NZ, NY, last, pos_ref, ra_ref, rb_ref, t_ref, s_ref, v_ref, h_ref, bot_ref,
                      lt_in, ls_in, pe_ref, qe_ref, pn_ref, qn_ref,
                      lt_ref, ls_ref, a0_ref, ae_ref, aw_ref, an_ref, as_ref, gl_ref, gr_ref, gg_ref, b_scr):
    x = rim_rows(NZ, NY, last, pos_ref, ra_ref, rb_ref, t_ref, s_ref, v_ref, h_ref, bot_ref)
    south, north = x["south"], x["north"]
    top = pl.ds(NY - 1, NZ, stride=NY)
    low = pl.ds(0, NZ, stride=NY)
    for n in range(2):
        gl_ref[pl.ds(2 * n, NZ, stride=8), :] = south(2 + n) - x["fs"][n]
        gl_ref[pl.ds(2 * n + 1, NZ, stride=8), :] = north(2 + n) + x["gn"][n]
        b_scr[pl.ds(2 * n, NZ, stride=8), :] = south(4)
        b_scr[pl.ds(2 * n + 1, NZ, stride=8), :] = north(4)
    zero = jnp.zeros((NZ, 128), F32)
    for n in range(4, 8):
        gl_ref[pl.ds(n, NZ, stride=8), :] = zero
        b_scr[pl.ds(n, NZ, stride=8), :] = zero
    above = g = jnp.zeros((8, 128), F32)
    for k in range(NZ):
        here, here8 = pl.ds(k * NY, NY), pl.ds(k * 8, 8)
        b = b_scr[here8, :]
        r = 1.0 / (1.0 + above + b - above * g)
        g = b * r
        above = b
        gr_ref[here8, :] = r
        gg_ref[here8, :] = g
        lt_ref[here, :] = lt_in[here, :]
        ls_ref[here, :] = ls_in[here, :]
        pe, qe = pe_ref[here, :], qe_ref[here, :]
        pn, qn = pn_ref[pl.ds(k * NY + 8, NY), :], qn_ref[pl.ds(k * NY + 8, NY), :]
        ps, qs = pn_ref[pl.ds(k * NY + 7, NY), :], qn_ref[pl.ds(k * NY + 7, NY), :]
        a0_ref[here, :] = 1.0 - (pe - roll(qe, 1)) - (pn - qs)
        ae_ref[here, :] = -qe
        aw_ref[here, :] = roll(pe, 1)
        an_ref[here, :] = -qn
        as_ref[here, :] = ps
    for n, ref in enumerate((lt_ref, ls_ref)):
        ref[low, :] = ref[low, :] + x["fs"][n]
        ref[top, :] = ref[top, :] - x["fn"][n]
    a0_ref[low, :] = a0_ref[low, :] + x["bes"]
    a0_ref[top, :] = a0_ref[top, :] - x["p15"]
    as_ref[low, :] = x["als"]
    an_ref[top, :] = -x["q15"]


def steps_kernel(NZ, NY, rw_ref, re_ref, own_ref, lt_ref, ls_ref, a0_ref, ae_ref, aw_ref, an_ref, as_ref,
                 r_ref, g_ref, gl_ref, gr_ref, gg_ref, bot_ref, to_ref, so_ref,
                 yt, ys, ct, cs, yte, yse, re_s, ge_s, yr, xt, xs, sems):
    shape = (NY, 128)
    PAD = NY + 16
    lane = lane_of(shape)
    lane8 = lane_of((8, 128))
    edge = (lane == 0) | (lane == 127)
    edge8 = (lane8 == 0) | (lane8 == 127)
    even, even8 = lax.rem(lane, 2) == 0, lax.rem(lane8, 2) == 0
    klane = lax.shift_right_logical(lane, 1).astype(F32)
    klane8 = lax.shift_right_logical(lane8, 1).astype(F32)

    def own(base, size):
        return own_ref[base : base + size, :]

    def ghost(base, size):
        ev = even if size == NY else even8
        return jnp.where(ev, roll(re_ref[base : base + size, :], -1), roll(rw_ref[base : base + size, :], 1))

    cb = 8 * NY
    bb = cb + 24

    def bottoms(base, size):
        ev = even if size == NY else even8
        sh = (size, 128)
        o, w, e = own(base, size), rw_ref[base : base + size, :], re_ref[base : base + size, :]

        def spread(x, col):
            return jnp.broadcast_to(x[:, col : col + 1], sh)

        mine = jnp.where(ev, spread(o, 127), spread(o, 0))
        theirs = jnp.where(ev, spread(e, 0), spread(w, 127))
        return mine, theirs

    bo, bg = bottoms(bb, NY)
    wo, wg = (klane < bo).astype(F32), (klane < bg).astype(F32)
    bot_edge = jnp.where(lane == 127, bg[:, 0:1], bg[:, 1:2])
    po = jnp.where(even, own(6 * NY, NY), 0.0)
    qo = jnp.where(even, own(7 * NY, NY), 0.0)
    pg = jnp.where(even, 0.0, ghost(6 * NY, NY))
    qg = jnp.where(even, 0.0, ghost(7 * NY, NY))
    alpha = wo * pg - wg * qo
    beta = wo * qg - wg * po
    corr = [alpha * ghost(n * NY, NY) + beta * own(n * NY, NY) for n in range(2)]
    glat = [ghost((2 + n) * NY, NY) - corr[n] for n in range(2)]
    gr, gg = ghost(4 * NY, NY), ghost(5 * NY, NY)

    bo8, bg8 = bottoms(bb + NY, 8)
    wo8, wg8 = (klane8 < bo8).astype(F32), (klane8 < bg8).astype(F32)
    co, cg = own(cb, 8), ghost(cb, 8)
    corner = wo8 * (ghost(cb + 8, 8) * cg + ghost(cb + 16, 8) * co) - wg8 * (own(cb + 8, 8) * co + own(cb + 16, 8) * cg)
    bot_rows = own(bb + NY, 8)
    bot = bot_ref[...]

    z, z8 = jnp.zeros(shape, F32), jnp.zeros((8, 128), F32)
    y0 = y1 = e0 = e1 = gp = gep = z
    yrow = ggp = z8
    for k in range(NZ):
        here, here8 = pl.ds(k * NY, NY), pl.ds(k * 8, 8)
        turn = 127 - 2 * k
        y0 = lt_ref[here, :] + jnp.where(edge, roll(corr[0], turn), 0.0) + gp * y0
        y1 = ls_ref[here, :] + jnp.where(edge, roll(corr[1], turn), 0.0) + gp * y1
        e0 = roll(glat[0], turn) + gep * e0
        e1 = roll(glat[1], turn) + gep * e1
        yrow = gl_ref[here8, :] + jnp.where(edge8, roll(corner, turn), 0.0) + ggp * yrow
        yt[here, :] = y0
        ys[here, :] = y1
        yte[here, :] = e0
        yse[here, :] = e1
        yr[here8, :] = yrow
        gep = roll(gg, turn)
        re_s[here, :] = roll(gr, turn)
        ge_s[here, :] = gep
        gp, ggp = g_ref[here, :], gg_ref[here8, :]

    x0 = x1 = e0 = e1 = z
    xr = z8
    for k in reversed(range(NZ)):
        here, here8 = pl.ds(k * NY, NY), pl.ds(k * 8, 8)
        inner = pl.ds(k * PAD + 8, NY)
        r, g = r_ref[here, :], g_ref[here, :]
        x0 = r * yt[here, :] + g * x0
        x1 = r * ys[here, :] + g * x1
        w = k < bot
        ct[inner, :] = jnp.where(w, x0, 0.0)
        cs[inner, :] = jnp.where(w, x1, 0.0)
        r, g = re_s[here, :], ge_s[here, :]
        e0 = r * yte[here, :] + g * e0
        e1 = r * yse[here, :] + g * e1
        we = k < bot_edge
        yte[here, :] = jnp.where(we, e0, 0.0)
        yse[here, :] = jnp.where(we, e1, 0.0)
        xr = gr_ref[here8, :] * yr[here8, :] + gg_ref[here8, :] * xr
        c = jnp.where(k < bot_rows, xr, 0.0)
        ct[pl.ds(k * PAD + 7, 1), :] = c[0:1, :]
        ct[pl.ds(k * PAD + 8 + NY, 1), :] = c[1:2, :]
        cs[pl.ds(k * PAD + 7, 1), :] = c[2:3, :]
        cs[pl.ds(k * PAD + 8 + NY, 1), :] = c[3:4, :]

    gp = y0 = y1 = z
    for k in range(NZ):
        here = pl.ds(k * NY, NY)
        turn = 127 - 2 * k
        al = roll(alpha, turn)
        a0 = a0_ref[here, :] + jnp.where(edge, roll(beta, turn), 0.0)
        ae = jnp.where(lane == 127, al, ae_ref[here, :])
        aw = jnp.where(lane == 0, al, aw_ref[here, :])
        an, as_ = an_ref[here, :], as_ref[here, :]
        ys_new = []
        for c_ref, e_ref in ((ct, yte), (cs, yse)):
            c = c_ref[pl.ds(k * PAD + 8, NY), :]
            rim = e_ref[here, :]
            east = jnp.where(lane == 127, rim, roll(c, -1))
            west = jnp.where(lane == 0, rim, roll(c, 1))
            ys_new.append(
                a0 * c + (ae * east + aw * west)
                + (an * c_ref[pl.ds(k * PAD + 9, NY), :] + as_ * c_ref[pl.ds(k * PAD + 7, NY), :])
            )
        y0 = ys_new[0] + gp * y0
        y1 = ys_new[1] + gp * y1
        yt[here, :] = y0
        ys[here, :] = y1
        gp = g_ref[here, :]

    x0 = x1 = z
    part = max(NZ // CHUNKS, 1)
    copies = []
    for k in reversed(range(NZ)):
        here = pl.ds(k * NY, NY)
        r, g = r_ref[here, :], g_ref[here, :]
        x0 = r * yt[here, :] + g * x0
        x1 = r * ys[here, :] + g * x1
        w = k < bot
        xt[here, :] = jnp.where(w, x0, 0.0)
        xs[here, :] = jnp.where(w, x1, 0.0)
        if k % part == 0:
            chunk = pl.ds(k * NY, part * NY)
            for n, (src, dst) in enumerate(((xt, to_ref), (xs, so_ref))):
                copy = pltpu.make_async_copy(src.at[chunk], dst.at[chunk], sems.at[n, k // part])
                copy.start()
                copies.append(copy)
    for copy in copies:
        copy.wait()


VM = pl.BlockSpec(memory_space=pltpu.VMEM)
SM = pl.BlockSpec(memory_space=pltpu.SMEM)
HB = pl.BlockSpec(memory_space=pltpu.HBM)
CHUNKS = 4


def vmem(*shape):
    return pltpu.VMEM(shape, F32)


def call(kernel, ins, outs, out_specs=None, scratch=(), cost=0):
    return pl.pallas_call(
        kernel,
        out_shape=outs,
        in_specs=ins,
        out_specs=out_specs or [VM] * len(outs),
        scratch_shapes=list(scratch),
        compiler_params=pltpu.CompilerParams(vmem_limit_bytes=40 << 20),
        cost_estimate=pl.CostEstimate(flops=cost, bytes_accessed=cost, transcendentals=0) if cost else None,
    )


def per_device(temp, salt, east_speed, north_speed, mixing_h, mixing_v, wet, bottom):
    NZ, NY, NX = temp.shape
    count_lat, count_lon = lax.axis_size("lat"), lax.axis_size("lon")
    last = count_lat - 1
    size = NZ * NY
    flat = vmem(size, NX)
    fields = [a.reshape(size, NX) for a in (temp, salt, east_speed, north_speed, mixing_h, mixing_v)]
    pos = lax.axis_index("lat").astype(jnp.int32).reshape(1)
    first, second = lat_routes(count_lon, count_lat)
    axes = ("lon", "lat")

    msg_a, msg_b, t, s, u, v, h, m, bot = call(
        functools.partial(rows_kernel, NZ, NY, last),
        [SM] + [HB] * 7,
        [vmem(NF * NZ + 8, NX)] * 2 + [vmem(size + 8, NX)] * 6 + [pltpu.VMEM((NY, NX), jnp.int32)],
        scratch=[pltpu.SemaphoreType.DMA((7,))],
    )(pos, *[pltpu.with_memory_space_constraint(a, pltpu.HBM) for a in fields], pltpu.with_memory_space_constraint(bottom, pltpu.HBM))
    ra = lax.ppermute(msg_a, axes, first)
    rb = lax.ppermute(msg_b, axes, second)
    lt, ls, pe, qe, pn, qn, r, g, pk = call(
        functools.partial(block_kernel, NZ, NY), [VM] * 7,
        [flat] * 4 + [vmem(size + 8, NX)] * 2 + [flat] * 2 + [vmem(8 * NY, NX)], cost=10_000_000,
    )(t, s, u, v, h, m, bot)
    (cols,) = call(
        functools.partial(columns_kernel, NZ, NY, last), [SM] + [VM] * 8, [vmem(8 * NY + 24 + NY + 8, NX)]
    )(pos, ra, rb, t, s, v, h, bot, pk)
    from_west = lax.ppermute(cols, "lon", [(i, (i + 1) % count_lon) for i in range(count_lon)])
    from_east = lax.ppermute(cols, "lon", [((i + 1) % count_lon, i) for i in range(count_lon)])
    ghost = vmem(NZ * 8, NX)
    lt, ls, a0, ae, aw, an, as_, gl, gr, gg = call(
        functools.partial(ghost_rows_kernel, NZ, NY, last), [SM] + [VM] * 13, [flat] * 7 + [ghost] * 3,
        scratch=[ghost], cost=10_000_000,
    )(pos, ra, rb, t, s, v, h, bot, lt, ls, pe, qe, pn, qn)
    pad = vmem(NZ * (NY + 16), NX)
    out = call(
        functools.partial(steps_kernel, NZ, NY), [VM] * 16,
        [jax.ShapeDtypeStruct((size, NX), F32)] * 2, out_specs=[HB] * 2,
        scratch=[flat] * 2 + [pad] * 2 + [flat] * 4 + [ghost] + [flat] * 2 + [pltpu.SemaphoreType.DMA((2, CHUNKS))],
    )(from_west, from_east, cols, lt, ls, a0, ae, aw, an, as_, r, g, gl, gr, gg, bot)
    return tuple(o.reshape(temp.shape) for o in out)


def solution(mesh):
    field = P(None, "lat", "lon")
    return jax.shard_map(
        per_device,
        mesh=mesh,
        in_specs=(field,) * 7 + (P("lat", "lon"),),
        out_specs=(field, field),
        check_vma=False,
    )
```

```python
import functools

import jax
import jax.numpy as jnp
from jax import lax
from jax.experimental import pallas as pl
from jax.experimental.pallas import tpu as pltpu
from jax.sharding import PartitionSpec as P

F32 = jnp.float32
NF = 7
NFIRST = 4


def lat_routes(count_lon, count_lat):
    first, second = [], []
    for i in range(count_lon):
        for j in range(count_lat):
            here = i * count_lat + j
            upward, downward = (first, second) if j % 2 else (second, first)
            if j == count_lat - 1:
                upward.append((here, (count_lon - 1 - i) * count_lat + j))
            else:
                upward.append((here, here + 1))
            if j > 0:
                downward.append((here, here - 1))
    return first, second


def lane_of(shape):
    return lax.broadcasted_iota(jnp.int32, shape, 1)


def row_of(shape):
    return lax.broadcasted_iota(jnp.int32, shape, 0)


def roll(x, shift, axis=1):
    size = x.shape[axis]
    if isinstance(shift, int):
        shift = shift % size
    return pltpu.roll(x, shift, axis)


def diagonal(NZ, even, odd):
    lev, lane = row_of((NZ, 128)), lane_of((NZ, 128))
    even = jnp.broadcast_to(even, (NZ, 128))
    odd = jnp.broadcast_to(odd, (NZ, 128))
    picked = jnp.where(lane == 2 * lev, even, jnp.where(lane == 2 * lev + 1, odd, 0.0))
    return jnp.sum(picked, axis=0, keepdims=True)


def in_turn(jobs, apart):
    running, waiting, step = [], list(jobs), 0
    while running or waiting:
        if waiting and step % apart == 0:
            running.append(waiting.pop(0))
        running = [job for job in running if next(job, "end") != "end"]
        step += 1


def upwind(speed, mix):
    return jnp.maximum(speed, 0.0) + mix, jnp.minimum(speed, 0.0) - mix


def rows_kernel(NZ, NY, last, pos_ref, *refs):
    sources, (a_ref, a2_ref, b_ref, tails_ref), kept, sems = refs[:7], refs[7:11], refs[11:18], refs[18]
    t_ref, s_ref, u_ref, v_ref, h_ref, m_ref, bot_ref = kept
    size = NZ * NY
    copies = []
    for n in (6, 0, 1, 2, 4, 3, 5):
        there = kept[n] if n == 6 else kept[n].at[pl.ds(0, size)]
        copies.append(pltpu.make_async_copy(sources[n], there, sems.at[n]))
        copies[-1].start()
    for n in range(6):
        kept[n][size:, :] = jnp.zeros((8, 128), F32)
    for copy in copies:
        copy.wait()
    j = lax.rem(pos_ref[0], last + 1)
    odd = lax.rem(j, 2) == 1
    lev = row_of((NZ, 128))
    lane = lane_of((NZ, 128))

    def message(row, inner, top):
        def at(ref, r):
            return ref[pl.ds(r, NZ, stride=NY), :]

        def sea(r):
            return (lev < bot_ref[r : r + 1, :]).astype(F32)

        w, w2 = sea(row), sea(inner)
        pe, qe = upwind(at(u_ref, row), at(h_ref, row))
        pe, qe = w * pe, w * qe
        east = jnp.where(lane < 127, roll(w, -1), 0.0)
        if top:
            pn, qn = upwind(at(v_ref, inner), at(h_ref, inner))
        else:
            pn, qn = upwind(at(v_ref, row), at(h_ref, row))
        both = w * w2
        cells, lats = [], []
        for ref in (t_ref, s_ref):
            c, c2 = w * at(ref, row), w2 * at(ref, inner)
            flux = east * (pe * c + qe * roll(c, -1))
            lat = c - flux + roll(flux, 1)
            if top:
                lat = lat + both * (pn * c2 + qn * c)
            else:
                lat = lat - both * (pn * c + qn * c2)
            cells.append(c)
            lats.append(lat)
        coupling = jnp.where(lev + 1 < bot_ref[row : row + 1, :], at(m_ref, row), 0.0)
        if top:
            po, qo = upwind(at(v_ref, row), at(h_ref, row))
            po, qo = w * po, w * qo
        else:
            po = qo = jnp.zeros_like(w)
        row8 = row_of((8, 128))
        tail = jnp.zeros((8, 128), F32)
        lines = [bot_ref[row : row + 1, :].astype(F32), diagonal(NZ, pe[:, 127:128], qe[:, 127:128])]
        lines += [diagonal(NZ, x[:, 127:128], x[:, 0:1]) for x in (cells + [po, qo] if top else cells)]
        for n, line in enumerate(lines):
            tail = jnp.where(row8 == n, jnp.broadcast_to(line, (8, 128)), tail)
        return cells + lats + [coupling, po, qo, tail]

    up = message(NY - 1, NY - 2, True)
    down = message(0, 1, False)
    for f in range(NF):
        value = jnp.where(odd, up[f], down[f])
        if f < NFIRST:
            a_ref[f * NZ : (f + 1) * NZ, :] = value
        else:
            a2_ref[(f - NFIRST) * NZ : (f - NFIRST + 1) * NZ, :] = value
        b_ref[f * NZ : (f + 1) * NZ, :] = jnp.where(odd, down[f], up[f])
    a_ref[NFIRST * NZ :, :] = jnp.where(odd, up[NF], down[NF])
    b_ref[NF * NZ :, :] = jnp.where(odd, down[NF], up[NF])
    tails_ref[0:8, :] = up[NF]
    tails_ref[8:16, :] = down[NF]

    @pl.when(j == last)
    def _():
        row8, lane8 = row_of((8, 128)), lane_of((8, 128))
        for ref, size in ((a_ref, NFIRST * NZ), (a2_ref, (NF - NFIRST) * NZ)):
            for r in range(0, size, 8):
                ref[r : r + 8, :] = jnp.take_along_axis(ref[r : r + 8, :], 127 - lane8, axis=1)
        x = a_ref[NFIRST * NZ :, :]
        swapped = jnp.where(lax.rem(lane8, 2) == 0, roll(x, -1), roll(x, 1))
        flipped = jnp.take_along_axis(x, 127 - lane8, axis=1)
        a_ref[NFIRST * NZ :, :] = jnp.where(row8 == 0, flipped, jnp.where(row8 == 1, x, swapped))


def block_kernel(NZ, NY, t_ref, s_ref, u_ref, v_ref, h_ref, m_ref, bot_ref,
                 lt_ref, ls_ref, pe_ref, qe_ref, pn_ref, qn_ref, r_ref, g_ref, pk_ref):
    shape = (NY, 128)
    lane, row = lane_of(shape), row_of(shape)
    bot = bot_ref[...]
    bot_e = jnp.where(lane < 127, roll(bot, -1), 0)
    bot_n = jnp.where(row < NY - 1, roll(bot, -1, 0), 0)
    pair = lax.shift_right_logical(lane, 1)
    zero = jnp.zeros(shape, F32)
    pn_ref[0:8, :] = jnp.zeros((8, 128), F32)
    qn_ref[0:8, :] = jnp.zeros((8, 128), F32)
    packed = [zero] * 8
    chain = [zero, zero]

    def level(k):
        here = pl.ds(k * NY, NY)
        next_row = pl.ds(k * NY + 1, NY)
        sea, sea_e, sea_n = k < bot, k < bot_e, k < bot_n
        cells = [jnp.where(sea, src[here, :], 0.0) for src in (t_ref, s_ref)]
        easts = [roll(c, -1) for c in cells]
        yield
        yield
        yield
        yield
        yield
        h = h_ref[here, :]
        pe, qe = upwind(u_ref[here, :], h)
        pn, qn = upwind(v_ref[here, :], h)
        pe, qe = jnp.where(sea, pe, 0.0), jnp.where(sea, qe, 0.0)
        both_n = sea & sea_n
        pem, qem = jnp.where(sea_e, pe, 0.0), jnp.where(sea_e, qe, 0.0)
        pnm, qnm = jnp.where(both_n, pn, 0.0), jnp.where(both_n, qn, 0.0)
        pe_ref[here, :] = pem
        qe_ref[here, :] = qem
        pn_ref[pl.ds(k * NY + 8, NY), :] = pnm
        qn_ref[pl.ds(k * NY + 8, NY), :] = qnm
        parts, wests, souths = [], [], []
        for src, c, ce in zip((t_ref, s_ref), cells, easts):
            cn = jnp.where(sea_n, src[next_row, :], 0.0)
            fe = pem * c + qem * ce
            fn = pnm * c + qnm * cn
            parts.append(c - fe - fn)
            wests.append(roll(fe, 1))
            souths.append(roll(fn, 1, 0))
        b = jnp.where(k + 1 < bot, m_ref[here, :], 0.0)
        above, g = chain
        r = 1.0 / (1.0 + above + b - above * g)
        g = b * r
        chain[:] = b, g
        r_ref[here, :] = r
        g_ref[here, :] = g
        first = [roll(x, 2 * k + 1) for x in cells + [r, g, pe, qe]]
        yield
        yield
        yield
        yield
        yield
        lats = [x + y + z for x, y, z in zip(parts, wests, souths)]
        lt_ref[here, :] = lats[0]
        ls_ref[here, :] = lats[1]
        moved = first[:2] + [roll(x, 2 * k + 1) for x in lats] + first[2:]
        yield
        yield
        yield
        yield
        yield
        mine = pair == k
        packed[:] = [jnp.where(mine, x, p) for x, p in zip(moved, packed)]

    in_turn([level(k) for k in range(NZ)], 1)
    for f in range(8):
        pk_ref[f * NY : (f + 1) * NY, :] = packed[f]


def rim_rows(NZ, NY, last, pos_ref, ra_ref, ra2_ref, rb_ref, t_ref, s_ref, v_ref, h_ref, bot_ref):
    j = lax.rem(pos_ref[0], last + 1)
    odd = lax.rem(j, 2) == 1
    normal = (j != last).astype(F32)
    lev = row_of((NZ, 128))

    def chips(f):
        ref, f = (ra_ref, f) if f < NFIRST else (ra2_ref, f - NFIRST)
        return ref[f * NZ : (f + 1) * NZ, :]

    def south(f):
        return jnp.where(odd, rb_ref[f * NZ : (f + 1) * NZ, :], chips(f))

    def north(f):
        return jnp.where(odd, chips(f), rb_ref[f * NZ : (f + 1) * NZ, :])

    bots = jnp.where(odd, rb_ref[NF * NZ :, :], ra_ref[NFIRST * NZ :, :])
    botn = jnp.where(odd, ra_ref[NFIRST * NZ :, :], rb_ref[NF * NZ :, :])
    levf = lev.astype(F32)
    ws = (levf < bots[0:1, :]).astype(F32)
    wn = (levf < botn[0:1, :]).astype(F32)
    w0 = (lev < bot_ref[0:1, :]).astype(F32)
    w15 = (lev < bot_ref[NY - 1 : NY, :]).astype(F32)
    top = pl.ds(NY - 1, NZ, stride=NY)
    low = pl.ds(0, NZ, stride=NY)
    p15, q15 = upwind(v_ref[top, :], h_ref[top, :])
    p15, q15 = w15 * wn * p15, w15 * wn * q15
    als, bes = w0 * south(5), w0 * south(6)
    pf, qf = w15 * north(5), w15 * north(6)
    res = dict(als=als, bes=bes, p15=p15, q15=q15, south=south, north=north)
    fs, fn, gn = [], [], []
    for n, ref in enumerate((t_ref, s_ref)):
        c0, c15 = w0 * ref[low, :], w15 * ref[top, :]
        cs, cn = south(n), north(n)
        fs.append(als * cs + bes * c0)
        own = p15 * c15 + q15 * cn
        fn.append(own)
        gn.append(normal * own - (pf * cn + qf * c15))
    res.update(fs=fs, fn=fn, gn=gn)
    return res


def columns_kernel(NZ, NY, last, pos_ref, ra_ref, rb_ref, tails_ref, bot_ref, pk_ref, a_ref, b_ref, own_ref):
    j = lax.rem(pos_ref[0], last + 1)
    odd, fold = lax.rem(j, 2) == 1, j == last
    odd_lon = lax.rem(lax.div(pos_ref[0], last + 1), 2) == 1
    urgent, other = ra_ref[NFIRST * NZ :, :], rb_ref[NF * NZ :, :]
    south, north = jnp.where(odd, other, urgent), jnp.where(odd, urgent, other)
    bot = bot_ref[...].astype(F32)
    up, down = tails_ref[0:8, :], tails_ref[8:16, :]
    lane1 = lane_of((1, 128))
    klane = lax.shift_right_logical(lane1, 1).astype(F32)

    def sea(levels):
        east, west = jnp.broadcast_to(levels[:, 127:128], (1, 128)), jnp.broadcast_to(levels[:, 0:1], (1, 128))
        return (klane < jnp.where(lax.rem(lane1, 2) == 0, east, west)).astype(F32)

    w0, wn = sea(bot[0:1, :]), sea(north[0:1, :])
    row8, lane8 = row_of((8, 128)), lane_of((8, 128))
    even8 = lax.rem(lane8, 2) == 0
    packed = [pk_ref[f * NY : (f + 1) * NY, :] for f in range(8)]
    row = row_of((NY, 128))
    for n in range(2):
        c = slice(2 + n, 3 + n)
        fs = w0 * (south[4:5, :] * south[c, :] + south[5:6, :] * down[c, :])
        fn = wn * (up[4:5, :] * up[c, :] + up[5:6, :] * north[c, :])
        packed[2 + n] = packed[2 + n] + jnp.where(row == 0, fs, jnp.where(row == NY - 1, -fn, 0.0))

    def four(a, b, c, d):
        return jnp.where(row8 == 0, a, jnp.where(row8 == 1, b, jnp.where(row8 == 2, c, d)))

    cells = four(south[2:3, :], north[2:3, :], south[3:4, :], north[3:4, :])
    es, en = south[1:2, :], north[1:2, :]
    e = jnp.where(lax.rem(row8, 2) == 0, jnp.broadcast_to(es, (8, 128)), jnp.broadcast_to(en, (8, 128)))
    mirrored = fold & (lax.rem(row8, 2) == 1)
    p = jnp.where(mirrored, jnp.where(even8, 0.0, roll(e, 1)), jnp.where(even8, e, 0.0))
    q = jnp.where(mirrored, jnp.where(even8, 0.0, e), jnp.where(even8, roll(e, -1), 0.0))
    bots, botn = jnp.broadcast_to(south[0:1, :], (8, 128)), jnp.broadcast_to(north[0:1, :], (8, 128))
    levels = jnp.where(lax.rem(row8, 2) == 0, bots, botn)
    for n, f in enumerate((0, 1, 6, 7)):
        own_ref[n * NY : (n + 1) * NY, :] = packed[f]
    base = 4 * NY
    own_ref[base : base + 8, :] = cells
    own_ref[base + 8 : base + 16, :] = p
    own_ref[base + 16 : base + 24, :] = q
    own_ref[base + 24 : base + 32, :] = levels

    lane = lane_of((NY, 128))
    even = lax.rem(lane, 2) == 0
    for n in range(4):
        f1, f2 = packed[2 * n], packed[2 * n + 1]
        to_east = jnp.where(even, f1, roll(f2, 1))
        to_west = jnp.where(even, roll(f1, -1), f2)
        if n == 0:
            to_east = jnp.where(lane >= 96, bot[:, 127:128], to_east)
            to_west = jnp.where(lane >= 96, bot[:, 0:1], to_west)
        a_ref[n * NY : (n + 1) * NY, :] = jnp.where(odd_lon, to_west, to_east)
        b_ref[n * NY : (n + 1) * NY, :] = jnp.where(odd_lon, to_east, to_west)
    corner = jnp.where(row8 < 4, cells, jnp.where(row8 < 6, p, q))
    to_east = jnp.where(lane8 >= 96, levels[:, 127:128], corner)
    to_west = jnp.where(lane8 >= 96, levels[:, 0:1], corner)
    a_ref[base : base + 8, :] = jnp.where(odd_lon, to_west, to_east)
    b_ref[base : base + 8, :] = jnp.where(odd_lon, to_east, to_west)


def ghost_rows_kernel(NZ, NY, last, pos_ref, ra_ref, ra2_ref, rb_ref, t_ref, s_ref, v_ref, h_ref, bot_ref,
                      lt_in, ls_in, pe_ref, qe_ref, pn_ref, qn_ref,
                      lt_ref, ls_ref, a0_ref, ae_ref, aw_ref, an_ref, as_ref, gl_ref, gr_ref, gg_ref, b_scr):
    x = rim_rows(NZ, NY, last, pos_ref, ra_ref, ra2_ref, rb_ref, t_ref, s_ref, v_ref, h_ref, bot_ref)
    south, north = x["south"], x["north"]
    top = pl.ds(NY - 1, NZ, stride=NY)
    low = pl.ds(0, NZ, stride=NY)
    for n in range(2):
        gl_ref[pl.ds(2 * n, NZ, stride=8), :] = south(2 + n) - x["fs"][n]
        gl_ref[pl.ds(2 * n + 1, NZ, stride=8), :] = north(2 + n) + x["gn"][n]
        b_scr[pl.ds(2 * n, NZ, stride=8), :] = south(4)
        b_scr[pl.ds(2 * n + 1, NZ, stride=8), :] = north(4)
    zero = jnp.zeros((NZ, 128), F32)
    for n in range(4, 8):
        gl_ref[pl.ds(n, NZ, stride=8), :] = zero
        b_scr[pl.ds(n, NZ, stride=8), :] = zero
    above = g = jnp.zeros((8, 128), F32)
    for k in range(NZ):
        here, here8 = pl.ds(k * NY, NY), pl.ds(k * 8, 8)
        b = b_scr[here8, :]
        r = 1.0 / (1.0 + above + b - above * g)
        g = b * r
        above = b
        gr_ref[here8, :] = r
        gg_ref[here8, :] = g
        lt_ref[here, :] = lt_in[here, :]
        ls_ref[here, :] = ls_in[here, :]
        pe, qe = pe_ref[here, :], qe_ref[here, :]
        pn, qn = pn_ref[pl.ds(k * NY + 8, NY), :], qn_ref[pl.ds(k * NY + 8, NY), :]
        ps, qs = pn_ref[pl.ds(k * NY + 7, NY), :], qn_ref[pl.ds(k * NY + 7, NY), :]
        a0_ref[here, :] = 1.0 - (pe - roll(qe, 1)) - (pn - qs)
        ae_ref[here, :] = -qe
        aw_ref[here, :] = roll(pe, 1)
        an_ref[here, :] = -qn
        as_ref[here, :] = ps
    for n, ref in enumerate((lt_ref, ls_ref)):
        ref[low, :] = ref[low, :] + x["fs"][n]
        ref[top, :] = ref[top, :] - x["fn"][n]
    a0_ref[low, :] = a0_ref[low, :] + x["bes"]
    a0_ref[top, :] = a0_ref[top, :] - x["p15"]
    as_ref[low, :] = x["als"]
    an_ref[top, :] = -x["q15"]


def steps_kernel(NZ, NY, last, pos_ref, ra_ref, rb_ref, own_ref, lt_ref, ls_ref, a0_ref, ae_ref, aw_ref, an_ref, as_ref,
                 r_ref, g_ref, gl_ref, gr_ref, gg_ref, bot_ref, to_ref, so_ref,
                 yt, ys, ct, cs, yte, yse, re_s, ge_s, yr, xt, xs, sems):
    shape = (NY, 128)
    PAD = NY + 16
    lane = lane_of(shape)
    lane8 = lane_of((8, 128))
    edge = (lane == 0) | (lane == 127)
    edge8 = (lane8 == 0) | (lane8 == 127)
    even, even8 = lax.rem(lane, 2) == 0, lax.rem(lane8, 2) == 0
    klane = lax.shift_right_logical(lane, 1).astype(F32)
    klane8 = lax.shift_right_logical(lane8, 1).astype(F32)

    odd_lon = lax.rem(lax.div(pos_ref[0], last + 1), 2) == 1
    base = 4 * NY

    def own(start, size):
        return own_ref[start : start + size, :]

    def received(start, size):
        a, b = ra_ref[start : start + size, :], rb_ref[start : start + size, :]
        return jnp.where(odd_lon, a, b), jnp.where(odd_lon, b, a)

    def spread(x, col, size):
        return jnp.broadcast_to(x[:, col : col + 1], (size, 128))

    ghosts = []
    for n in range(4):
        west, east = received(n * NY, NY)
        if n == 0:
            bg_east, bg_west = spread(east, 96, NY), spread(west, 96, NY)
        ghosts.append(jnp.where(even, east, roll(west, 1)))
        ghosts.append(jnp.where(even, roll(east, -1), west))
    west, east = received(base, 8)
    bg8 = jnp.where(even8, spread(east, 96, 8), spread(west, 96, 8))
    corners = jnp.where(even8, roll(east, -1), roll(west, 1))
    bot = bot_ref[...]
    botf = bot.astype(F32)
    bo = jnp.where(even, spread(botf, 127, NY), spread(botf, 0, NY))
    bg = jnp.where(even, bg_east, bg_west)
    wo, wg = (klane < bo).astype(F32), (klane < bg).astype(F32)
    bot_edge = jnp.where(lane == 127, bg_east, bg_west)
    po = jnp.where(even, own(2 * NY, NY), 0.0)
    qo = jnp.where(even, own(3 * NY, NY), 0.0)
    pg = jnp.where(even, 0.0, ghosts[6])
    qg = jnp.where(even, 0.0, ghosts[7])
    alpha = wo * pg - wg * qo
    beta = wo * qg - wg * po
    corr = [alpha * ghosts[n] + beta * own(n * NY, NY) for n in range(2)]
    glat = [ghosts[2 + n] - corr[n] for n in range(2)]
    gr, gg = ghosts[4], ghosts[5]

    bot_rows = own(base + 24, 8)
    bo8 = jnp.where(even8, spread(bot_rows, 127, 8), spread(bot_rows, 0, 8))
    wo8, wg8 = (klane8 < bo8).astype(F32), (klane8 < bg8).astype(F32)
    first_two = row_of((8, 128)) < 2
    pg8 = jnp.where(first_two, roll(corners, -4, 0), roll(corners, -2, 0))
    qg8 = jnp.where(first_two, roll(corners, -6, 0), roll(corners, -4, 0))
    co, po8, qo8 = own(base, 8), own(base + 8, 8), own(base + 16, 8)
    corner = wo8 * (pg8 * corners + qg8 * co) - wg8 * (po8 * co + qo8 * corners)

    z, z8 = jnp.zeros(shape, F32), jnp.zeros((8, 128), F32)
    y0 = y1 = e0 = e1 = gp = gep = z
    yrow = ggp = z8
    for k in range(NZ):
        here, here8 = pl.ds(k * NY, NY), pl.ds(k * 8, 8)
        turn = 127 - 2 * k
        y0 = lt_ref[here, :] + jnp.where(edge, roll(corr[0], turn), 0.0) + gp * y0
        y1 = ls_ref[here, :] + jnp.where(edge, roll(corr[1], turn), 0.0) + gp * y1
        e0 = roll(glat[0], turn) + gep * e0
        e1 = roll(glat[1], turn) + gep * e1
        yrow = gl_ref[here8, :] + jnp.where(edge8, roll(corner, turn), 0.0) + ggp * yrow
        yt[here, :] = y0
        ys[here, :] = y1
        yte[here, :] = e0
        yse[here, :] = e1
        yr[here8, :] = yrow
        gep = roll(gg, turn)
        re_s[here, :] = roll(gr, turn)
        ge_s[here, :] = gep
        gp, ggp = g_ref[here, :], gg_ref[here8, :]

    x0 = x1 = e0 = e1 = z
    xr = z8
    for k in reversed(range(NZ)):
        here, here8 = pl.ds(k * NY, NY), pl.ds(k * 8, 8)
        inner = pl.ds(k * PAD + 8, NY)
        r, g = r_ref[here, :], g_ref[here, :]
        x0 = r * yt[here, :] + g * x0
        x1 = r * ys[here, :] + g * x1
        w = k < bot
        ct[inner, :] = jnp.where(w, x0, 0.0)
        cs[inner, :] = jnp.where(w, x1, 0.0)
        r, g = re_s[here, :], ge_s[here, :]
        e0 = r * yte[here, :] + g * e0
        e1 = r * yse[here, :] + g * e1
        we = k < bot_edge
        yte[here, :] = jnp.where(we, e0, 0.0)
        yse[here, :] = jnp.where(we, e1, 0.0)
        xr = gr_ref[here8, :] * yr[here8, :] + gg_ref[here8, :] * xr
        c = jnp.where(k < bot_rows, xr, 0.0)
        ct[pl.ds(k * PAD + 7, 1), :] = c[0:1, :]
        ct[pl.ds(k * PAD + 8 + NY, 1), :] = c[1:2, :]
        cs[pl.ds(k * PAD + 7, 1), :] = c[2:3, :]
        cs[pl.ds(k * PAD + 8 + NY, 1), :] = c[3:4, :]

    gp = y0 = y1 = z
    for k in range(NZ):
        here = pl.ds(k * NY, NY)
        turn = 127 - 2 * k
        al = roll(alpha, turn)
        a0 = a0_ref[here, :] + jnp.where(edge, roll(beta, turn), 0.0)
        ae = jnp.where(lane == 127, al, ae_ref[here, :])
        aw = jnp.where(lane == 0, al, aw_ref[here, :])
        an, as_ = an_ref[here, :], as_ref[here, :]
        ys_new = []
        for c_ref, e_ref in ((ct, yte), (cs, yse)):
            c = c_ref[pl.ds(k * PAD + 8, NY), :]
            rim = e_ref[here, :]
            east = jnp.where(lane == 127, rim, roll(c, -1))
            west = jnp.where(lane == 0, rim, roll(c, 1))
            ys_new.append(
                a0 * c + (ae * east + aw * west)
                + (an * c_ref[pl.ds(k * PAD + 9, NY), :] + as_ * c_ref[pl.ds(k * PAD + 7, NY), :])
            )
        y0 = ys_new[0] + gp * y0
        y1 = ys_new[1] + gp * y1
        yt[here, :] = y0
        ys[here, :] = y1
        gp = g_ref[here, :]

    x0 = x1 = z
    part = max(NZ // CHUNKS, 1)
    copies = []
    for k in reversed(range(NZ)):
        here = pl.ds(k * NY, NY)
        r, g = r_ref[here, :], g_ref[here, :]
        x0 = r * yt[here, :] + g * x0
        x1 = r * ys[here, :] + g * x1
        w = k < bot
        xt[here, :] = jnp.where(w, x0, 0.0)
        xs[here, :] = jnp.where(w, x1, 0.0)
        if k % part == 0:
            chunk = pl.ds(k * NY, part * NY)
            for n, (src, dst) in enumerate(((xt, to_ref), (xs, so_ref))):
                copy = pltpu.make_async_copy(src.at[chunk], dst.at[chunk], sems.at[n, k // part])
                copy.start()
                copies.append(copy)
    for copy in copies:
        copy.wait()


VM = pl.BlockSpec(memory_space=pltpu.VMEM)
SM = pl.BlockSpec(memory_space=pltpu.SMEM)
HB = pl.BlockSpec(memory_space=pltpu.HBM)
CHUNKS = 4


def vmem(*shape):
    return pltpu.VMEM(shape, F32)


def call(kernel, ins, outs, out_specs=None, scratch=(), cost=0):
    return pl.pallas_call(
        kernel,
        out_shape=outs,
        in_specs=ins,
        out_specs=out_specs or [VM] * len(outs),
        scratch_shapes=list(scratch),
        compiler_params=pltpu.CompilerParams(vmem_limit_bytes=40 << 20),
        cost_estimate=pl.CostEstimate(flops=cost, bytes_accessed=cost, transcendentals=0) if cost else None,
    )


def per_device(temp, salt, east_speed, north_speed, mixing_h, mixing_v, wet, bottom):
    NZ, NY, NX = temp.shape
    count_lat, count_lon = lax.axis_size("lat"), lax.axis_size("lon")
    last = count_lat - 1
    size = NZ * NY
    flat = vmem(size, NX)
    fields = [a.reshape(size, NX) for a in (temp, salt, east_speed, north_speed, mixing_h, mixing_v)]
    axes = ("lon", "lat")
    pos = lax.axis_index(axes).astype(jnp.int32).reshape(1)
    first, second = lat_routes(count_lon, count_lat)

    msg_a, msg_a2, msg_b, tails, t, s, u, v, h, m, bot = call(
        functools.partial(rows_kernel, NZ, NY, last),
        [SM] + [HB] * 7,
        [vmem(NFIRST * NZ + 8, NX), vmem((NF - NFIRST) * NZ, NX), vmem(NF * NZ + 8, NX), vmem(16, NX)]
        + [vmem(size + 8, NX)] * 6 + [pltpu.VMEM((NY, NX), jnp.int32)],
        scratch=[pltpu.SemaphoreType.DMA((7,))],
    )(pos, *[pltpu.with_memory_space_constraint(a, pltpu.HBM) for a in fields], pltpu.with_memory_space_constraint(bottom, pltpu.HBM))
    ra = lax.ppermute(msg_a, axes, first)
    rb = lax.ppermute(msg_b, axes, second)
    upward = [(x, y) for x, y in first if NFIRST < 5 or x % count_lat % 2]
    ra2 = lax.ppermute(msg_a2, axes, upward)
    lt, ls, pe, qe, pn, qn, r, g, pk = call(
        functools.partial(block_kernel, NZ, NY), [VM] * 7,
        [flat] * 4 + [vmem(size + 8, NX)] * 2 + [flat] * 2 + [vmem(8 * NY, NX)], cost=10_000_000,
    )(t, s, u, v, h, m, bot)
    col_msg = vmem(4 * NY + 8, NX)
    cols_a, cols_b, own = call(
        functools.partial(columns_kernel, NZ, NY, last), [SM] + [VM] * 5, [col_msg] * 2 + [vmem(4 * NY + 32, NX)]
    )(pos, ra, rb, tails, bot, pk)
    ca = lax.ppermute(cols_a, "lon", [(i, i ^ 1) for i in range(count_lon)])
    cb = lax.ppermute(cols_b, "lon", [(i, (i + 1 if i % 2 else i - 1) % count_lon) for i in range(count_lon)])
    ghost = vmem(NZ * 8, NX)
    lt, ls, a0, ae, aw, an, as_, gl, gr, gg = call(
        functools.partial(ghost_rows_kernel, NZ, NY, last), [SM] + [VM] * 14, [flat] * 7 + [ghost] * 3,
        scratch=[ghost], cost=10_000_000,
    )(pos, ra, ra2, rb, t, s, v, h, bot, lt, ls, pe, qe, pn, qn)
    pad = vmem(NZ * (NY + 16), NX)
    out = call(
        functools.partial(steps_kernel, NZ, NY, last), [SM] + [VM] * 16,
        [jax.ShapeDtypeStruct((size, NX), F32)] * 2, out_specs=[HB] * 2,
        scratch=[flat] * 2 + [pad] * 2 + [flat] * 4 + [ghost] + [flat] * 2 + [pltpu.SemaphoreType.DMA((2, CHUNKS))],
    )(pos, ca, cb, own, lt, ls, a0, ae, aw, an, as_, r, g, gl, gr, gg, bot)
    return tuple(o.reshape(temp.shape) for o in out)


def solution(mesh):
    field = P(None, "lat", "lon")
    return jax.shard_map(
        per_device,
        mesh=mesh,
        in_specs=(field,) * 7 + (P("lat", "lon"),),
        out_specs=(field, field),
        check_vma=False,
    )
```

```python
import functools

import jax
import jax.numpy as jnp
from jax import lax
from jax.experimental import pallas as pl
from jax.experimental.pallas import tpu as pltpu
from jax.sharding import PartitionSpec as P

F32 = jnp.float32
NF = 7
NFIRST = 4


def lat_routes(count_lon, count_lat):
    first, second = [], []
    for i in range(count_lon):
        for j in range(count_lat):
            here = i * count_lat + j
            upward, downward = (first, second) if j % 2 else (second, first)
            if j == count_lat - 1:
                upward.append((here, (count_lon - 1 - i) * count_lat + j))
            else:
                upward.append((here, here + 1))
            if j > 0:
                downward.append((here, here - 1))
    return first, second


def lane_of(shape):
    return lax.broadcasted_iota(jnp.int32, shape, 1)


def row_of(shape):
    return lax.broadcasted_iota(jnp.int32, shape, 0)


def roll(x, shift, axis=1):
    size = x.shape[axis]
    if isinstance(shift, int):
        shift = shift % size
    return pltpu.roll(x, shift, axis)


def diagonal(NZ, even, odd):
    lev, lane = row_of((NZ, 128)), lane_of((NZ, 128))
    even = jnp.broadcast_to(even, (NZ, 128))
    odd = jnp.broadcast_to(odd, (NZ, 128))
    picked = jnp.where(lane == 2 * lev, even, jnp.where(lane == 2 * lev + 1, odd, 0.0))
    return jnp.sum(picked, axis=0, keepdims=True)


def inward(NZ):
    half = NZ // 2
    return [pair for k in range(half) for pair in ((k, 0), (NZ - 1 - k, 1))]


def meet(top, bottom):
    (rt, gt, yt), (rb, gb, yb) = top, bottom
    xt, xb, d = rt * yt, rb * yb, 1.0 / (1.0 - gt * gb)
    return (xb + gb * xt) * d, (xt + gt * xb) * d


def in_turn(jobs, apart):
    running, waiting, step = [], list(jobs), 0
    while running or waiting:
        if waiting and step % apart == 0:
            running.append(waiting.pop(0))
        running = [job for job in running if next(job, "end") != "end"]
        step += 1


def upwind(speed, mix):
    return jnp.maximum(speed, 0.0) + mix, jnp.minimum(speed, 0.0) - mix


def rows_kernel(NZ, NY, last, pos_ref, *refs):
    sources, (a_ref, a2_ref, b_ref, tails_ref), kept, sems = refs[:7], refs[7:11], refs[11:18], refs[18]
    t_ref, s_ref, u_ref, v_ref, h_ref, m_ref, bot_ref = kept
    size = NZ * NY
    copies = []
    for n in (6, 0, 1, 2, 4, 3, 5):
        there = kept[n] if n == 6 else kept[n].at[pl.ds(0, size)]
        copies.append(pltpu.make_async_copy(sources[n], there, sems.at[n]))
        copies[-1].start()
    for n in range(6):
        kept[n][size:, :] = jnp.zeros((8, 128), F32)
    for copy in copies:
        copy.wait()
    j = lax.rem(pos_ref[0], last + 1)
    odd = lax.rem(j, 2) == 1
    lev = row_of((NZ, 128))
    lane = lane_of((NZ, 128))

    def message(row, inner, top):
        def at(ref, r):
            return ref[pl.ds(r, NZ, stride=NY), :]

        def sea(r):
            return (lev < bot_ref[r : r + 1, :]).astype(F32)

        w, w2 = sea(row), sea(inner)
        pe, qe = upwind(at(u_ref, row), at(h_ref, row))
        pe, qe = w * pe, w * qe
        east = jnp.where(lane < 127, roll(w, -1), 0.0)
        if top:
            pn, qn = upwind(at(v_ref, inner), at(h_ref, inner))
        else:
            pn, qn = upwind(at(v_ref, row), at(h_ref, row))
        both = w * w2
        cells, lats = [], []
        for ref in (t_ref, s_ref):
            c, c2 = w * at(ref, row), w2 * at(ref, inner)
            flux = east * (pe * c + qe * roll(c, -1))
            lat = c - flux + roll(flux, 1)
            if top:
                lat = lat + both * (pn * c2 + qn * c)
            else:
                lat = lat - both * (pn * c + qn * c2)
            cells.append(c)
            lats.append(lat)
        coupling = jnp.where(lev + 1 < bot_ref[row : row + 1, :], at(m_ref, row), 0.0)
        if top:
            po, qo = upwind(at(v_ref, row), at(h_ref, row))
            po, qo = w * po, w * qo
        else:
            po = qo = jnp.zeros_like(w)
        row8 = row_of((8, 128))
        tail = jnp.zeros((8, 128), F32)
        lines = [bot_ref[row : row + 1, :].astype(F32), diagonal(NZ, pe[:, 127:128], qe[:, 127:128])]
        lines += [diagonal(NZ, x[:, 127:128], x[:, 0:1]) for x in (cells + [po, qo] if top else cells)]
        for n, line in enumerate(lines):
            tail = jnp.where(row8 == n, jnp.broadcast_to(line, (8, 128)), tail)
        return cells + lats + [coupling, po, qo, tail]

    up = message(NY - 1, NY - 2, True)
    down = message(0, 1, False)
    for f in range(NF):
        value = jnp.where(odd, up[f], down[f])
        if f < NFIRST:
            a_ref[f * NZ : (f + 1) * NZ, :] = value
        else:
            a2_ref[(f - NFIRST) * NZ : (f - NFIRST + 1) * NZ, :] = value
        b_ref[f * NZ : (f + 1) * NZ, :] = jnp.where(odd, down[f], up[f])
    a_ref[NFIRST * NZ :, :] = jnp.where(odd, up[NF], down[NF])
    b_ref[NF * NZ :, :] = jnp.where(odd, down[NF], up[NF])
    tails_ref[0:8, :] = up[NF]
    tails_ref[8:16, :] = down[NF]

    @pl.when(j == last)
    def _():
        row8, lane8 = row_of((8, 128)), lane_of((8, 128))
        for ref, size in ((a_ref, NFIRST * NZ), (a2_ref, (NF - NFIRST) * NZ)):
            for r in range(0, size, 8):
                ref[r : r + 8, :] = jnp.take_along_axis(ref[r : r + 8, :], 127 - lane8, axis=1)
        x = a_ref[NFIRST * NZ :, :]
        swapped = jnp.where(lax.rem(lane8, 2) == 0, roll(x, -1), roll(x, 1))
        flipped = jnp.take_along_axis(x, 127 - lane8, axis=1)
        a_ref[NFIRST * NZ :, :] = jnp.where(row8 == 0, flipped, jnp.where(row8 == 1, x, swapped))


def block_kernel(NZ, NY, t_ref, s_ref, u_ref, v_ref, h_ref, m_ref, bot_ref,
                 lt_ref, ls_ref, pe_ref, qe_ref, pn_ref, qn_ref, r_ref, g_ref, pk_ref):
    shape = (NY, 128)
    lane, row = lane_of(shape), row_of(shape)
    bot = bot_ref[...]
    bot_e = jnp.where(lane < 127, roll(bot, -1), 0)
    bot_n = jnp.where(row < NY - 1, roll(bot, -1, 0), 0)
    pair = lax.shift_right_logical(lane, 1)
    zero = jnp.zeros(shape, F32)
    pn_ref[0:8, :] = jnp.zeros((8, 128), F32)
    qn_ref[0:8, :] = jnp.zeros((8, 128), F32)
    packed = [zero] * 8
    chains = [[zero, zero], [zero, zero]]

    def coupling(k):
        return jnp.where(k + 1 < bot, m_ref[pl.ds(k * NY, NY), :], 0.0)

    def level(k, side):
        here = pl.ds(k * NY, NY)
        next_row = pl.ds(k * NY + 1, NY)
        sea, sea_e, sea_n = k < bot, k < bot_e, k < bot_n
        cells = [jnp.where(sea, src[here, :], 0.0) for src in (t_ref, s_ref)]
        easts = [roll(c, -1) for c in cells]
        yield
        yield
        yield
        yield
        yield
        h = h_ref[here, :]
        pe, qe = upwind(u_ref[here, :], h)
        pn, qn = upwind(v_ref[here, :], h)
        pe, qe = jnp.where(sea, pe, 0.0), jnp.where(sea, qe, 0.0)
        both_n = sea & sea_n
        pem, qem = jnp.where(sea_e, pe, 0.0), jnp.where(sea_e, qe, 0.0)
        pnm, qnm = jnp.where(both_n, pn, 0.0), jnp.where(both_n, qn, 0.0)
        pe_ref[here, :] = pem
        qe_ref[here, :] = qem
        pn_ref[pl.ds(k * NY + 8, NY), :] = pnm
        qn_ref[pl.ds(k * NY + 8, NY), :] = qnm
        parts, wests, souths = [], [], []
        for src, c, ce in zip((t_ref, s_ref), cells, easts):
            cn = jnp.where(sea_n, src[next_row, :], 0.0)
            fe = pem * c + qem * ce
            fn = pnm * c + qnm * cn
            parts.append(c - fe - fn)
            wests.append(roll(fe, 1))
            souths.append(roll(fn, 1, 0))
        b = coupling(k - side)
        behind, g = chains[side]
        r = 1.0 / (1.0 + behind + b - behind * g)
        g = b * r
        chains[side][:] = b, g
        r_ref[here, :] = r
        g_ref[here, :] = g
        first = [roll(x, 2 * k + 1) for x in cells + [r, g, pe, qe]]
        yield
        yield
        yield
        yield
        yield
        lats = [x + y + z for x, y, z in zip(parts, wests, souths)]
        lt_ref[here, :] = lats[0]
        ls_ref[here, :] = lats[1]
        moved = first[:2] + [roll(x, 2 * k + 1) for x in lats] + first[2:]
        yield
        yield
        yield
        yield
        yield
        mine = pair == k
        packed[:] = [jnp.where(mine, x, p) for x, p in zip(moved, packed)]

    in_turn([level(*pair) for pair in inward(NZ)], 1)
    for f in range(8):
        pk_ref[f * NY : (f + 1) * NY, :] = packed[f]


def rim_rows(NZ, NY, last, pos_ref, ra_ref, ra2_ref, rb_ref, t_ref, s_ref, v_ref, h_ref, bot_ref):
    j = lax.rem(pos_ref[0], last + 1)
    odd = lax.rem(j, 2) == 1
    normal = (j != last).astype(F32)
    lev = row_of((NZ, 128))

    def chips(f):
        ref, f = (ra_ref, f) if f < NFIRST else (ra2_ref, f - NFIRST)
        return ref[f * NZ : (f + 1) * NZ, :]

    def south(f):
        return jnp.where(odd, rb_ref[f * NZ : (f + 1) * NZ, :], chips(f))

    def north(f):
        return jnp.where(odd, chips(f), rb_ref[f * NZ : (f + 1) * NZ, :])

    bots = jnp.where(odd, rb_ref[NF * NZ :, :], ra_ref[NFIRST * NZ :, :])
    botn = jnp.where(odd, ra_ref[NFIRST * NZ :, :], rb_ref[NF * NZ :, :])
    levf = lev.astype(F32)
    ws = (levf < bots[0:1, :]).astype(F32)
    wn = (levf < botn[0:1, :]).astype(F32)
    w0 = (lev < bot_ref[0:1, :]).astype(F32)
    w15 = (lev < bot_ref[NY - 1 : NY, :]).astype(F32)
    top = pl.ds(NY - 1, NZ, stride=NY)
    low = pl.ds(0, NZ, stride=NY)
    p15, q15 = upwind(v_ref[top, :], h_ref[top, :])
    p15, q15 = w15 * wn * p15, w15 * wn * q15
    als, bes = w0 * south(5), w0 * south(6)
    pf, qf = w15 * north(5), w15 * north(6)
    res = dict(als=als, bes=bes, p15=p15, q15=q15, south=south, north=north)
    fs, fn, gn = [], [], []
    for n, ref in enumerate((t_ref, s_ref)):
        c0, c15 = w0 * ref[low, :], w15 * ref[top, :]
        cs, cn = south(n), north(n)
        fs.append(als * cs + bes * c0)
        own = p15 * c15 + q15 * cn
        fn.append(own)
        gn.append(normal * own - (pf * cn + qf * c15))
    res.update(fs=fs, fn=fn, gn=gn)
    return res


def columns_kernel(NZ, NY, last, pos_ref, ra_ref, rb_ref, tails_ref, bot_ref, pk_ref, a_ref, b_ref, own_ref):
    j = lax.rem(pos_ref[0], last + 1)
    odd, fold = lax.rem(j, 2) == 1, j == last
    odd_lon = lax.rem(lax.div(pos_ref[0], last + 1), 2) == 1
    urgent, other = ra_ref[NFIRST * NZ :, :], rb_ref[NF * NZ :, :]
    south, north = jnp.where(odd, other, urgent), jnp.where(odd, urgent, other)
    bot = bot_ref[...].astype(F32)
    up, down = tails_ref[0:8, :], tails_ref[8:16, :]
    lane1 = lane_of((1, 128))
    klane = lax.shift_right_logical(lane1, 1).astype(F32)

    def sea(levels):
        east, west = jnp.broadcast_to(levels[:, 127:128], (1, 128)), jnp.broadcast_to(levels[:, 0:1], (1, 128))
        return (klane < jnp.where(lax.rem(lane1, 2) == 0, east, west)).astype(F32)

    w0, wn = sea(bot[0:1, :]), sea(north[0:1, :])
    row8, lane8 = row_of((8, 128)), lane_of((8, 128))
    even8 = lax.rem(lane8, 2) == 0
    packed = [pk_ref[f * NY : (f + 1) * NY, :] for f in range(8)]
    row = row_of((NY, 128))
    for n in range(2):
        c = slice(2 + n, 3 + n)
        fs = w0 * (south[4:5, :] * south[c, :] + south[5:6, :] * down[c, :])
        fn = wn * (up[4:5, :] * up[c, :] + up[5:6, :] * north[c, :])
        packed[2 + n] = packed[2 + n] + jnp.where(row == 0, fs, jnp.where(row == NY - 1, -fn, 0.0))

    def four(a, b, c, d):
        return jnp.where(row8 == 0, a, jnp.where(row8 == 1, b, jnp.where(row8 == 2, c, d)))

    cells = four(south[2:3, :], north[2:3, :], south[3:4, :], north[3:4, :])
    es, en = south[1:2, :], north[1:2, :]
    e = jnp.where(lax.rem(row8, 2) == 0, jnp.broadcast_to(es, (8, 128)), jnp.broadcast_to(en, (8, 128)))
    mirrored = fold & (lax.rem(row8, 2) == 1)
    p = jnp.where(mirrored, jnp.where(even8, 0.0, roll(e, 1)), jnp.where(even8, e, 0.0))
    q = jnp.where(mirrored, jnp.where(even8, 0.0, e), jnp.where(even8, roll(e, -1), 0.0))
    bots, botn = jnp.broadcast_to(south[0:1, :], (8, 128)), jnp.broadcast_to(north[0:1, :], (8, 128))
    levels = jnp.where(lax.rem(row8, 2) == 0, bots, botn)
    for n, f in enumerate((0, 1, 6, 7)):
        own_ref[n * NY : (n + 1) * NY, :] = packed[f]
    base = 4 * NY
    own_ref[base : base + 8, :] = cells
    own_ref[base + 8 : base + 16, :] = p
    own_ref[base + 16 : base + 24, :] = q
    own_ref[base + 24 : base + 32, :] = levels

    lane = lane_of((NY, 128))
    even = lax.rem(lane, 2) == 0
    for n in range(4):
        f1, f2 = packed[2 * n], packed[2 * n + 1]
        to_east = jnp.where(even, f1, roll(f2, 1))
        to_west = jnp.where(even, roll(f1, -1), f2)
        if n == 0:
            to_east = jnp.where(lane >= 96, bot[:, 127:128], to_east)
            to_west = jnp.where(lane >= 96, bot[:, 0:1], to_west)
        a_ref[n * NY : (n + 1) * NY, :] = jnp.where(odd_lon, to_west, to_east)
        b_ref[n * NY : (n + 1) * NY, :] = jnp.where(odd_lon, to_east, to_west)
    corner = jnp.where(row8 < 4, cells, jnp.where(row8 < 6, p, q))
    to_east = jnp.where(lane8 >= 96, levels[:, 127:128], corner)
    to_west = jnp.where(lane8 >= 96, levels[:, 0:1], corner)
    a_ref[base : base + 8, :] = jnp.where(odd_lon, to_west, to_east)
    b_ref[base : base + 8, :] = jnp.where(odd_lon, to_east, to_west)


def ghost_rows_kernel(NZ, NY, last, pos_ref, ra_ref, ra2_ref, rb_ref, t_ref, s_ref, v_ref, h_ref, bot_ref,
                      lt_in, ls_in, pe_ref, qe_ref, pn_ref, qn_ref,
                      lt_ref, ls_ref, a0_ref, ae_ref, aw_ref, an_ref, as_ref, gl_ref, gr_ref, gg_ref, b_scr):
    x = rim_rows(NZ, NY, last, pos_ref, ra_ref, ra2_ref, rb_ref, t_ref, s_ref, v_ref, h_ref, bot_ref)
    south, north = x["south"], x["north"]
    top = pl.ds(NY - 1, NZ, stride=NY)
    low = pl.ds(0, NZ, stride=NY)
    for n in range(2):
        gl_ref[pl.ds(2 * n, NZ, stride=8), :] = south(2 + n) - x["fs"][n]
        gl_ref[pl.ds(2 * n + 1, NZ, stride=8), :] = north(2 + n) + x["gn"][n]
        b_scr[pl.ds(2 * n, NZ, stride=8), :] = south(4)
        b_scr[pl.ds(2 * n + 1, NZ, stride=8), :] = north(4)
    zero = jnp.zeros((NZ, 128), F32)
    for n in range(4, 8):
        gl_ref[pl.ds(n, NZ, stride=8), :] = zero
        b_scr[pl.ds(n, NZ, stride=8), :] = zero
    z8 = jnp.zeros((8, 128), F32)
    chains = [[z8, z8], [z8, z8]]
    for k, side in inward(NZ):
        here, here8 = pl.ds(k * NY, NY), pl.ds(k * 8, 8)
        b = b_scr[pl.ds((k - side) * 8, 8), :]
        behind, g = chains[side]
        r = 1.0 / (1.0 + behind + b - behind * g)
        g = b * r
        chains[side][:] = b, g
        gr_ref[here8, :] = r
        gg_ref[here8, :] = g
        lt_ref[here, :] = lt_in[here, :]
        ls_ref[here, :] = ls_in[here, :]
        pe, qe = pe_ref[here, :], qe_ref[here, :]
        pn, qn = pn_ref[pl.ds(k * NY + 8, NY), :], qn_ref[pl.ds(k * NY + 8, NY), :]
        ps, qs = pn_ref[pl.ds(k * NY + 7, NY), :], qn_ref[pl.ds(k * NY + 7, NY), :]
        a0_ref[here, :] = 1.0 - (pe - roll(qe, 1)) - (pn - qs)
        ae_ref[here, :] = -qe
        aw_ref[here, :] = roll(pe, 1)
        an_ref[here, :] = -qn
        as_ref[here, :] = ps
    for n, ref in enumerate((lt_ref, ls_ref)):
        ref[low, :] = ref[low, :] + x["fs"][n]
        ref[top, :] = ref[top, :] - x["fn"][n]
    a0_ref[low, :] = a0_ref[low, :] + x["bes"]
    a0_ref[top, :] = a0_ref[top, :] - x["p15"]
    as_ref[low, :] = x["als"]
    an_ref[top, :] = -x["q15"]


def steps_kernel(NZ, NY, last, pos_ref, ra_ref, rb_ref, own_ref, lt_ref, ls_ref, a0_ref, ae_ref, aw_ref, an_ref, as_ref,
                 r_ref, g_ref, gl_ref, gr_ref, gg_ref, bot_ref, to_ref, so_ref,
                 yt, ys, ct, cs, yte, yse, re_s, ge_s, yr, xt, xs, sems):
    shape = (NY, 128)
    PAD = NY + 16
    lane = lane_of(shape)
    lane8 = lane_of((8, 128))
    edge = (lane == 0) | (lane == 127)
    edge8 = (lane8 == 0) | (lane8 == 127)
    even, even8 = lax.rem(lane, 2) == 0, lax.rem(lane8, 2) == 0
    klane = lax.shift_right_logical(lane, 1).astype(F32)
    klane8 = lax.shift_right_logical(lane8, 1).astype(F32)

    odd_lon = lax.rem(lax.div(pos_ref[0], last + 1), 2) == 1
    base = 4 * NY

    def own(start, size):
        return own_ref[start : start + size, :]

    def received(start, size):
        a, b = ra_ref[start : start + size, :], rb_ref[start : start + size, :]
        return jnp.where(odd_lon, a, b), jnp.where(odd_lon, b, a)

    def spread(x, col, size):
        return jnp.broadcast_to(x[:, col : col + 1], (size, 128))

    ghosts = []
    for n in range(4):
        west, east = received(n * NY, NY)
        if n == 0:
            bg_east, bg_west = spread(east, 96, NY), spread(west, 96, NY)
        ghosts.append(jnp.where(even, east, roll(west, 1)))
        ghosts.append(jnp.where(even, roll(east, -1), west))
    west, east = received(base, 8)
    bg8 = jnp.where(even8, spread(east, 96, 8), spread(west, 96, 8))
    corners = jnp.where(even8, roll(east, -1), roll(west, 1))
    bot = bot_ref[...]
    botf = bot.astype(F32)
    bo = jnp.where(even, spread(botf, 127, NY), spread(botf, 0, NY))
    bg = jnp.where(even, bg_east, bg_west)
    wo, wg = (klane < bo).astype(F32), (klane < bg).astype(F32)
    bot_edge = jnp.where(lane == 127, bg_east, bg_west)
    po = jnp.where(even, own(2 * NY, NY), 0.0)
    qo = jnp.where(even, own(3 * NY, NY), 0.0)
    pg = jnp.where(even, 0.0, ghosts[6])
    qg = jnp.where(even, 0.0, ghosts[7])
    alpha = wo * pg - wg * qo
    beta = wo * qg - wg * po
    corr = [alpha * ghosts[n] + beta * own(n * NY, NY) for n in range(2)]
    glat = [ghosts[2 + n] - corr[n] for n in range(2)]
    gr, gg = ghosts[4], ghosts[5]

    bot_rows = own(base + 24, 8)
    bo8 = jnp.where(even8, spread(bot_rows, 127, 8), spread(bot_rows, 0, 8))
    wo8, wg8 = (klane8 < bo8).astype(F32), (klane8 < bg8).astype(F32)
    first_two = row_of((8, 128)) < 2
    pg8 = jnp.where(first_two, roll(corners, -4, 0), roll(corners, -2, 0))
    qg8 = jnp.where(first_two, roll(corners, -6, 0), roll(corners, -4, 0))
    co, po8, qo8 = own(base, 8), own(base + 8, 8), own(base + 16, 8)
    corner = wo8 * (pg8 * corners + qg8 * co) - wg8 * (po8 * co + qo8 * corners)

    z, z8 = jnp.zeros(shape, F32), jnp.zeros((8, 128), F32)
    state = [(z, z, z, z, z, z, z8, z8)] * 2
    last_r = [None, None]
    for k, side in inward(NZ):
        y0, y1, e0, e1, gp, gep, yrow, ggp = state[side]
        here, here8 = pl.ds(k * NY, NY), pl.ds(k * 8, 8)
        turn = 127 - 2 * k
        y0 = lt_ref[here, :] + jnp.where(edge, roll(corr[0], turn), 0.0) + gp * y0
        y1 = ls_ref[here, :] + jnp.where(edge, roll(corr[1], turn), 0.0) + gp * y1
        e0 = roll(glat[0], turn) + gep * e0
        e1 = roll(glat[1], turn) + gep * e1
        yrow = gl_ref[here8, :] + jnp.where(edge8, roll(corner, turn), 0.0) + ggp * yrow
        yt[here, :] = y0
        ys[here, :] = y1
        yte[here, :] = e0
        yse[here, :] = e1
        yr[here8, :] = yrow
        gep = roll(gg, turn)
        rep = roll(gr, turn)
        re_s[here, :] = rep
        ge_s[here, :] = gep
        gp, ggp = g_ref[here, :], gg_ref[here8, :]
        state[side] = y0, y1, e0, e1, gp, gep, yrow, ggp
        if abs(2 * k + 1 - NZ) == 1:
            last_r[side] = r_ref[here, :], rep, gr_ref[here8, :]

    found = []
    for y, r, g in ((0, 0, 4), (1, 0, 4), (2, 1, 5), (3, 1, 5), (6, 2, 7)):
        found.append(meet(*[(last_r[side][r], state[side][g], state[side][y]) for side in range(2)]))
    state = [tuple(x[side] for x in found) for side in range(2)]
    for k, side in reversed(inward(NZ)):
        x0, x1, e0, e1, xr = state[side]
        here, here8 = pl.ds(k * NY, NY), pl.ds(k * 8, 8)
        inner = pl.ds(k * PAD + 8, NY)
        r, g = r_ref[here, :], g_ref[here, :]
        x0 = r * yt[here, :] + g * x0
        x1 = r * ys[here, :] + g * x1
        w = k < bot
        ct[inner, :] = jnp.where(w, x0, 0.0)
        cs[inner, :] = jnp.where(w, x1, 0.0)
        r, g = re_s[here, :], ge_s[here, :]
        e0 = r * yte[here, :] + g * e0
        e1 = r * yse[here, :] + g * e1
        we = k < bot_edge
        yte[here, :] = jnp.where(we, e0, 0.0)
        yse[here, :] = jnp.where(we, e1, 0.0)
        xr = gr_ref[here8, :] * yr[here8, :] + gg_ref[here8, :] * xr
        state[side] = x0, x1, e0, e1, xr
        c = jnp.where(k < bot_rows, xr, 0.0)
        ct[pl.ds(k * PAD + 7, 1), :] = c[0:1, :]
        ct[pl.ds(k * PAD + 8 + NY, 1), :] = c[1:2, :]
        cs[pl.ds(k * PAD + 7, 1), :] = c[2:3, :]
        cs[pl.ds(k * PAD + 8 + NY, 1), :] = c[3:4, :]

    state = [(z, z, z)] * 2
    for k, side in inward(NZ):
        y0, y1, gp = state[side]
        here = pl.ds(k * NY, NY)
        turn = 127 - 2 * k
        al = roll(alpha, turn)
        a0 = a0_ref[here, :] + jnp.where(edge, roll(beta, turn), 0.0)
        ae = jnp.where(lane == 127, al, ae_ref[here, :])
        aw = jnp.where(lane == 0, al, aw_ref[here, :])
        an, as_ = an_ref[here, :], as_ref[here, :]
        ys_new = []
        for c_ref, e_ref in ((ct, yte), (cs, yse)):
            c = c_ref[pl.ds(k * PAD + 8, NY), :]
            rim = e_ref[here, :]
            east = jnp.where(lane == 127, rim, roll(c, -1))
            west = jnp.where(lane == 0, rim, roll(c, 1))
            ys_new.append(
                a0 * c + (ae * east + aw * west)
                + (an * c_ref[pl.ds(k * PAD + 9, NY), :] + as_ * c_ref[pl.ds(k * PAD + 7, NY), :])
            )
        y0 = ys_new[0] + gp * y0
        y1 = ys_new[1] + gp * y1
        yt[here, :] = y0
        ys[here, :] = y1
        state[side] = y0, y1, g_ref[here, :]

    middle = [pl.ds((NZ // 2 - 1 + side) * NY, NY) for side in range(2)]
    found = [meet(*[(r_ref[middle[side], :], state[side][2], state[side][n]) for side in range(2)]) for n in range(2)]
    state = [tuple(x[side] for x in found) for side in range(2)]
    part = max(NZ // CHUNKS, 1)
    copies = []
    for k, side in reversed(inward(NZ)):
        x0, x1 = state[side]
        here = pl.ds(k * NY, NY)
        r, g = r_ref[here, :], g_ref[here, :]
        x0 = r * yt[here, :] + g * x0
        x1 = r * ys[here, :] + g * x1
        w = k < bot
        xt[here, :] = jnp.where(w, x0, 0.0)
        xs[here, :] = jnp.where(w, x1, 0.0)
        state[side] = x0, x1
        if (k + side) % part == 0:
            chunk = pl.ds((k // part) * part * NY, part * NY)
            for n, (src, dst) in enumerate(((xt, to_ref), (xs, so_ref))):
                copy = pltpu.make_async_copy(src.at[chunk], dst.at[chunk], sems.at[n, k // part])
                copy.start()
                copies.append(copy)
    for copy in copies:
        copy.wait()


VM = pl.BlockSpec(memory_space=pltpu.VMEM)
SM = pl.BlockSpec(memory_space=pltpu.SMEM)
HB = pl.BlockSpec(memory_space=pltpu.HBM)
CHUNKS = 4


def vmem(*shape):
    return pltpu.VMEM(shape, F32)


def call(kernel, ins, outs, out_specs=None, scratch=(), cost=0):
    return pl.pallas_call(
        kernel,
        out_shape=outs,
        in_specs=ins,
        out_specs=out_specs or [VM] * len(outs),
        scratch_shapes=list(scratch),
        compiler_params=pltpu.CompilerParams(vmem_limit_bytes=40 << 20),
        cost_estimate=pl.CostEstimate(flops=cost, bytes_accessed=cost, transcendentals=0) if cost else None,
    )


def per_device(temp, salt, east_speed, north_speed, mixing_h, mixing_v, wet, bottom):
    NZ, NY, NX = temp.shape
    count_lat, count_lon = lax.axis_size("lat"), lax.axis_size("lon")
    last = count_lat - 1
    size = NZ * NY
    flat = vmem(size, NX)
    fields = [a.reshape(size, NX) for a in (temp, salt, east_speed, north_speed, mixing_h, mixing_v)]
    axes = ("lon", "lat")
    pos = lax.axis_index(axes).astype(jnp.int32).reshape(1)
    first, second = lat_routes(count_lon, count_lat)

    msg_a, msg_a2, msg_b, tails, t, s, u, v, h, m, bot = call(
        functools.partial(rows_kernel, NZ, NY, last),
        [SM] + [HB] * 7,
        [vmem(NFIRST * NZ + 8, NX), vmem((NF - NFIRST) * NZ, NX), vmem(NF * NZ + 8, NX), vmem(16, NX)]
        + [vmem(size + 8, NX)] * 6 + [pltpu.VMEM((NY, NX), jnp.int32)],
        scratch=[pltpu.SemaphoreType.DMA((7,))],
    )(pos, *[pltpu.with_memory_space_constraint(a, pltpu.HBM) for a in fields], pltpu.with_memory_space_constraint(bottom, pltpu.HBM))
    ra = lax.ppermute(msg_a, axes, first)
    rb = lax.ppermute(msg_b, axes, second)
    upward = [(x, y) for x, y in first if NFIRST < 5 or x % count_lat % 2]
    ra2 = lax.ppermute(msg_a2, axes, upward)
    lt, ls, pe, qe, pn, qn, r, g, pk = call(
        functools.partial(block_kernel, NZ, NY), [VM] * 7,
        [flat] * 4 + [vmem(size + 8, NX)] * 2 + [flat] * 2 + [vmem(8 * NY, NX)], cost=10_000_000,
    )(t, s, u, v, h, m, bot)
    col_msg = vmem(4 * NY + 8, NX)
    cols_a, cols_b, own = call(
        functools.partial(columns_kernel, NZ, NY, last), [SM] + [VM] * 5, [col_msg] * 2 + [vmem(4 * NY + 32, NX)]
    )(pos, ra, rb, tails, bot, pk)
    ca = lax.ppermute(cols_a, "lon", [(i, i ^ 1) for i in range(count_lon)])
    cb = lax.ppermute(cols_b, "lon", [(i, (i + 1 if i % 2 else i - 1) % count_lon) for i in range(count_lon)])
    ghost = vmem(NZ * 8, NX)
    lt, ls, a0, ae, aw, an, as_, gl, gr, gg = call(
        functools.partial(ghost_rows_kernel, NZ, NY, last), [SM] + [VM] * 14, [flat] * 7 + [ghost] * 3,
        scratch=[ghost], cost=10_000_000,
    )(pos, ra, ra2, rb, t, s, v, h, bot, lt, ls, pe, qe, pn, qn)
    pad = vmem(NZ * (NY + 16), NX)
    out = call(
        functools.partial(steps_kernel, NZ, NY, last), [SM] + [VM] * 16,
        [jax.ShapeDtypeStruct((size, NX), F32)] * 2, out_specs=[HB] * 2,
        scratch=[flat] * 2 + [pad] * 2 + [flat] * 4 + [ghost] + [flat] * 2 + [pltpu.SemaphoreType.DMA((2, CHUNKS))],
    )(pos, ca, cb, own, lt, ls, a0, ae, aw, an, as_, r, g, gl, gr, gg, bot)
    return tuple(o.reshape(temp.shape) for o in out)


def solution(mesh):
    field = P(None, "lat", "lon")
    return jax.shard_map(
        per_device,
        mesh=mesh,
        in_specs=(field,) * 7 + (P("lat", "lon"),),
        out_specs=(field, field),
        check_vma=False,
    )
```

```python
import functools

import jax
import jax.numpy as jnp
from jax import lax
from jax.experimental import pallas as pl
from jax.experimental.pallas import tpu as pltpu
from jax.sharding import PartitionSpec as P

F32 = jnp.float32
NF = 7
NFIRST = 4


def lat_routes(count_lon, count_lat):
    first, second = [], []
    for i in range(count_lon):
        for j in range(count_lat):
            here = i * count_lat + j
            upward, downward = (first, second) if j % 2 else (second, first)
            if j == count_lat - 1:
                upward.append((here, (count_lon - 1 - i) * count_lat + j))
            else:
                upward.append((here, here + 1))
            if j > 0:
                downward.append((here, here - 1))
    return first, second


def lane_of(shape):
    return lax.broadcasted_iota(jnp.int32, shape, 1)


def row_of(shape):
    return lax.broadcasted_iota(jnp.int32, shape, 0)


def roll(x, shift, axis=1):
    size = x.shape[axis]
    if isinstance(shift, int):
        shift = shift % size
    return pltpu.roll(x, shift, axis)


def diagonal(NZ, even, odd):
    lev, lane = row_of((NZ, 128)), lane_of((NZ, 128))
    even = jnp.broadcast_to(even, (NZ, 128))
    odd = jnp.broadcast_to(odd, (NZ, 128))
    picked = jnp.where(lane == 2 * lev, even, jnp.where(lane == 2 * lev + 1, odd, 0.0))
    return jnp.sum(picked, axis=0, keepdims=True)


def inward(NZ):
    half = NZ // 2
    return [pair for k in range(half) for pair in ((k, 0), (NZ - 1 - k, 1))]


def meet(top, bottom):
    (rt, gt, yt), (rb, gb, yb) = top, bottom
    xt, xb, d = rt * yt, rb * yb, 1.0 / (1.0 - gt * gb)
    return (xb + gb * xt) * d, (xt + gt * xb) * d


def in_turn(jobs, apart):
    running, waiting, step = [], list(jobs), 0
    while running or waiting:
        if waiting and step % apart == 0:
            running.append(waiting.pop(0))
        running = [job for job in running if next(job, "end") != "end"]
        step += 1


def upwind(speed, mix):
    return jnp.maximum(speed, 0.0) + mix, jnp.minimum(speed, 0.0) - mix


def rows_kernel(NZ, NY, last, pos_ref, *refs):
    sources, (a_ref, a2_ref, b_ref, tails_ref), kept, sems = refs[:7], refs[7:11], refs[11:18], refs[18]
    t_ref, s_ref, u_ref, v_ref, h_ref, m_ref, bot_ref = kept
    copies = [pltpu.make_async_copy(sources[6], bot_ref, sems.at[6, 0])]
    for n in (0, 1, 2, 4, 3, 5):
        one = n in (2, 5)
        for side, start in enumerate((0, NY - 1 if one else NY - 2)):
            rows = pl.ds(start, 1 if one else 2)
            copies.append(pltpu.make_async_copy(sources[n].at[:, rows, :], kept[n].at[:, rows, :], sems.at[n, side]))
    for copy in copies:
        copy.start()
    for copy in copies:
        copy.wait()
    j = lax.rem(pos_ref[0], last + 1)
    odd = lax.rem(j, 2) == 1
    lev = row_of((NZ, 128))
    lane = lane_of((NZ, 128))

    def message(row, inner, top):
        def at(ref, r):
            return ref[:, r, :]

        def sea(r):
            return (lev < bot_ref[r : r + 1, :]).astype(F32)

        w, w2 = sea(row), sea(inner)
        pe, qe = upwind(at(u_ref, row), at(h_ref, row))
        pe, qe = w * pe, w * qe
        east = jnp.where(lane < 127, roll(w, -1), 0.0)
        if top:
            pn, qn = upwind(at(v_ref, inner), at(h_ref, inner))
        else:
            pn, qn = upwind(at(v_ref, row), at(h_ref, row))
        both = w * w2
        cells, lats = [], []
        for ref in (t_ref, s_ref):
            c, c2 = w * at(ref, row), w2 * at(ref, inner)
            flux = east * (pe * c + qe * roll(c, -1))
            lat = c - flux + roll(flux, 1)
            if top:
                lat = lat + both * (pn * c2 + qn * c)
            else:
                lat = lat - both * (pn * c + qn * c2)
            cells.append(c)
            lats.append(lat)
        coupling = jnp.where(lev + 1 < bot_ref[row : row + 1, :], at(m_ref, row), 0.0)
        if top:
            po, qo = upwind(at(v_ref, row), at(h_ref, row))
            po, qo = w * po, w * qo
        else:
            po = qo = jnp.zeros_like(w)
        row8 = row_of((8, 128))
        tail = jnp.zeros((8, 128), F32)
        lines = [bot_ref[row : row + 1, :].astype(F32), diagonal(NZ, pe[:, 127:128], qe[:, 127:128])]
        lines += [diagonal(NZ, x[:, 127:128], x[:, 0:1]) for x in (cells + [po, qo] if top else cells)]
        for n, line in enumerate(lines):
            tail = jnp.where(row8 == n, jnp.broadcast_to(line, (8, 128)), tail)
        return cells + lats + [coupling, po, qo, tail]

    up = message(NY - 1, NY - 2, True)
    down = message(0, 1, False)
    for f in range(NF):
        value = jnp.where(odd, up[f], down[f])
        if f < NFIRST:
            a_ref[f * NZ : (f + 1) * NZ, :] = value
        else:
            a2_ref[(f - NFIRST) * NZ : (f - NFIRST + 1) * NZ, :] = value
        b_ref[f * NZ : (f + 1) * NZ, :] = jnp.where(odd, down[f], up[f])
    a_ref[NFIRST * NZ :, :] = jnp.where(odd, up[NF], down[NF])
    b_ref[NF * NZ :, :] = jnp.where(odd, down[NF], up[NF])
    tails_ref[0:8, :] = up[NF]
    tails_ref[8:16, :] = down[NF]

    @pl.when(j == last)
    def _():
        row8, lane8 = row_of((8, 128)), lane_of((8, 128))
        for ref, size in ((a_ref, NFIRST * NZ), (a2_ref, (NF - NFIRST) * NZ)):
            for r in range(0, size, 8):
                ref[r : r + 8, :] = jnp.take_along_axis(ref[r : r + 8, :], 127 - lane8, axis=1)
        x = a_ref[NFIRST * NZ :, :]
        swapped = jnp.where(lax.rem(lane8, 2) == 0, roll(x, -1), roll(x, 1))
        flipped = jnp.take_along_axis(x, 127 - lane8, axis=1)
        a_ref[NFIRST * NZ :, :] = jnp.where(row8 == 0, flipped, jnp.where(row8 == 1, x, swapped))


def block_kernel(NZ, NY, t_ref, s_ref, u_ref, v_ref, h_ref, m_ref, bot_ref,
                 lt_ref, ls_ref, pe_ref, qe_ref, pn_ref, qn_ref, r_ref, g_ref, pk_ref):
    shape = (NY, 128)
    lane, row = lane_of(shape), row_of(shape)
    bot = bot_ref[...]
    bot_e = jnp.where(lane < 127, roll(bot, -1), 0)
    bot_n = jnp.where(row < NY - 1, roll(bot, -1, 0), 0)
    pair = lax.shift_right_logical(lane, 1)
    zero = jnp.zeros(shape, F32)
    pn_ref[0:8, :] = jnp.zeros((8, 128), F32)
    qn_ref[0:8, :] = jnp.zeros((8, 128), F32)
    packed = [zero] * 8
    chains = [[zero, zero], [zero, zero]]

    def coupling(k):
        return jnp.where(k + 1 < bot, m_ref[pl.ds(k * NY, NY), :], 0.0)

    def level(k, side):
        here = pl.ds(k * NY, NY)
        next_row = pl.ds(k * NY + 1, NY)
        sea, sea_e, sea_n = k < bot, k < bot_e, k < bot_n
        cells = [jnp.where(sea, src[here, :], 0.0) for src in (t_ref, s_ref)]
        easts = [roll(c, -1) for c in cells]
        yield
        yield
        yield
        yield
        yield
        h = h_ref[here, :]
        pe, qe = upwind(u_ref[here, :], h)
        pn, qn = upwind(v_ref[here, :], h)
        pe, qe = jnp.where(sea, pe, 0.0), jnp.where(sea, qe, 0.0)
        both_n = sea & sea_n
        pem, qem = jnp.where(sea_e, pe, 0.0), jnp.where(sea_e, qe, 0.0)
        pnm, qnm = jnp.where(both_n, pn, 0.0), jnp.where(both_n, qn, 0.0)
        pe_ref[here, :] = pem
        qe_ref[here, :] = qem
        pn_ref[pl.ds(k * NY + 8, NY), :] = pnm
        qn_ref[pl.ds(k * NY + 8, NY), :] = qnm
        parts, wests, souths = [], [], []
        for src, c, ce in zip((t_ref, s_ref), cells, easts):
            cn = src[next_row, :] if k < NZ - 1 else roll(src[here, :], -1, 0)
            cn = jnp.where(sea_n, cn, 0.0)
            fe = pem * c + qem * ce
            fn = pnm * c + qnm * cn
            parts.append(c - fe - fn)
            wests.append(roll(fe, 1))
            souths.append(roll(fn, 1, 0))
        b = coupling(k - side)
        behind, g = chains[side]
        r = 1.0 / (1.0 + behind + b - behind * g)
        g = b * r
        chains[side][:] = b, g
        r_ref[here, :] = r
        g_ref[here, :] = g
        first = [roll(x, 2 * k + 1) for x in cells + [r, g, pe, qe]]
        yield
        yield
        yield
        yield
        yield
        lats = [x + y + z for x, y, z in zip(parts, wests, souths)]
        lt_ref[here, :] = lats[0]
        ls_ref[here, :] = lats[1]
        moved = first[:2] + [roll(x, 2 * k + 1) for x in lats] + first[2:]
        yield
        yield
        yield
        yield
        yield
        mine = pair == k
        packed[:] = [jnp.where(mine, x, p) for x, p in zip(moved, packed)]

    in_turn([level(*pair) for pair in inward(NZ)], 1)
    for f in range(8):
        pk_ref[f * NY : (f + 1) * NY, :] = packed[f]


def rim_rows(NZ, NY, last, pos_ref, ra_ref, ra2_ref, rb_ref, t_ref, s_ref, v_ref, h_ref, bot_ref):
    j = lax.rem(pos_ref[0], last + 1)
    odd = lax.rem(j, 2) == 1
    normal = (j != last).astype(F32)
    lev = row_of((NZ, 128))

    def chips(f):
        ref, f = (ra_ref, f) if f < NFIRST else (ra2_ref, f - NFIRST)
        return ref[f * NZ : (f + 1) * NZ, :]

    def south(f):
        return jnp.where(odd, rb_ref[f * NZ : (f + 1) * NZ, :], chips(f))

    def north(f):
        return jnp.where(odd, chips(f), rb_ref[f * NZ : (f + 1) * NZ, :])

    bots = jnp.where(odd, rb_ref[NF * NZ :, :], ra_ref[NFIRST * NZ :, :])
    botn = jnp.where(odd, ra_ref[NFIRST * NZ :, :], rb_ref[NF * NZ :, :])
    levf = lev.astype(F32)
    ws = (levf < bots[0:1, :]).astype(F32)
    wn = (levf < botn[0:1, :]).astype(F32)
    w0 = (lev < bot_ref[0:1, :]).astype(F32)
    w15 = (lev < bot_ref[NY - 1 : NY, :]).astype(F32)
    top = pl.ds(NY - 1, NZ, stride=NY)
    low = pl.ds(0, NZ, stride=NY)
    p15, q15 = upwind(v_ref[top, :], h_ref[top, :])
    p15, q15 = w15 * wn * p15, w15 * wn * q15
    als, bes = w0 * south(5), w0 * south(6)
    pf, qf = w15 * north(5), w15 * north(6)
    res = dict(als=als, bes=bes, p15=p15, q15=q15, south=south, north=north)
    fs, fn, gn = [], [], []
    for n, ref in enumerate((t_ref, s_ref)):
        c0, c15 = w0 * ref[low, :], w15 * ref[top, :]
        cs, cn = south(n), north(n)
        fs.append(als * cs + bes * c0)
        own = p15 * c15 + q15 * cn
        fn.append(own)
        gn.append(normal * own - (pf * cn + qf * c15))
    res.update(fs=fs, fn=fn, gn=gn)
    return res


def columns_kernel(NZ, NY, last, pos_ref, ra_ref, rb_ref, tails_ref, bot_ref, pk_ref, a_ref, b_ref, own_ref):
    j = lax.rem(pos_ref[0], last + 1)
    odd, fold = lax.rem(j, 2) == 1, j == last
    odd_lon = lax.rem(lax.div(pos_ref[0], last + 1), 2) == 1
    urgent, other = ra_ref[NFIRST * NZ :, :], rb_ref[NF * NZ :, :]
    south, north = jnp.where(odd, other, urgent), jnp.where(odd, urgent, other)
    bot = bot_ref[...].astype(F32)
    up, down = tails_ref[0:8, :], tails_ref[8:16, :]
    lane1 = lane_of((1, 128))
    klane = lax.shift_right_logical(lane1, 1).astype(F32)

    def sea(levels):
        east, west = jnp.broadcast_to(levels[:, 127:128], (1, 128)), jnp.broadcast_to(levels[:, 0:1], (1, 128))
        return (klane < jnp.where(lax.rem(lane1, 2) == 0, east, west)).astype(F32)

    w0, wn = sea(bot[0:1, :]), sea(north[0:1, :])
    row8, lane8 = row_of((8, 128)), lane_of((8, 128))
    even8 = lax.rem(lane8, 2) == 0
    packed = [pk_ref[f * NY : (f + 1) * NY, :] for f in range(8)]
    row = row_of((NY, 128))
    for n in range(2):
        c = slice(2 + n, 3 + n)
        fs = w0 * (south[4:5, :] * south[c, :] + south[5:6, :] * down[c, :])
        fn = wn * (up[4:5, :] * up[c, :] + up[5:6, :] * north[c, :])
        packed[2 + n] = packed[2 + n] + jnp.where(row == 0, fs, jnp.where(row == NY - 1, -fn, 0.0))

    def four(a, b, c, d):
        return jnp.where(row8 == 0, a, jnp.where(row8 == 1, b, jnp.where(row8 == 2, c, d)))

    cells = four(south[2:3, :], north[2:3, :], south[3:4, :], north[3:4, :])
    es, en = south[1:2, :], north[1:2, :]
    e = jnp.where(lax.rem(row8, 2) == 0, jnp.broadcast_to(es, (8, 128)), jnp.broadcast_to(en, (8, 128)))
    mirrored = fold & (lax.rem(row8, 2) == 1)
    p = jnp.where(mirrored, jnp.where(even8, 0.0, roll(e, 1)), jnp.where(even8, e, 0.0))
    q = jnp.where(mirrored, jnp.where(even8, 0.0, e), jnp.where(even8, roll(e, -1), 0.0))
    bots, botn = jnp.broadcast_to(south[0:1, :], (8, 128)), jnp.broadcast_to(north[0:1, :], (8, 128))
    levels = jnp.where(lax.rem(row8, 2) == 0, bots, botn)
    for n, f in enumerate((0, 1, 6, 7)):
        own_ref[n * NY : (n + 1) * NY, :] = packed[f]
    base = 4 * NY
    own_ref[base : base + 8, :] = cells
    own_ref[base + 8 : base + 16, :] = p
    own_ref[base + 16 : base + 24, :] = q
    own_ref[base + 24 : base + 32, :] = levels

    lane = lane_of((NY, 128))
    even = lax.rem(lane, 2) == 0
    for n in range(4):
        f1, f2 = packed[2 * n], packed[2 * n + 1]
        to_east = jnp.where(even, f1, roll(f2, 1))
        to_west = jnp.where(even, roll(f1, -1), f2)
        if n == 0:
            to_east = jnp.where(lane >= 96, bot[:, 127:128], to_east)
            to_west = jnp.where(lane >= 96, bot[:, 0:1], to_west)
        a_ref[n * NY : (n + 1) * NY, :] = jnp.where(odd_lon, to_west, to_east)
        b_ref[n * NY : (n + 1) * NY, :] = jnp.where(odd_lon, to_east, to_west)
    corner = jnp.where(row8 < 4, cells, jnp.where(row8 < 6, p, q))
    to_east = jnp.where(lane8 >= 96, levels[:, 127:128], corner)
    to_west = jnp.where(lane8 >= 96, levels[:, 0:1], corner)
    a_ref[base : base + 8, :] = jnp.where(odd_lon, to_west, to_east)
    b_ref[base : base + 8, :] = jnp.where(odd_lon, to_east, to_west)


def ghost_rows_kernel(NZ, NY, last, pos_ref, ra_ref, ra2_ref, rb_ref, t_ref, s_ref, v_ref, h_ref, bot_ref,
                      lt_in, ls_in, pe_ref, qe_ref, pn_ref, qn_ref,
                      lt_ref, ls_ref, a0_ref, ae_ref, aw_ref, an_ref, as_ref, gl_ref, gr_ref, gg_ref, b_scr):
    x = rim_rows(NZ, NY, last, pos_ref, ra_ref, ra2_ref, rb_ref, t_ref, s_ref, v_ref, h_ref, bot_ref)
    south, north = x["south"], x["north"]
    top = pl.ds(NY - 1, NZ, stride=NY)
    low = pl.ds(0, NZ, stride=NY)
    for n in range(2):
        gl_ref[pl.ds(2 * n, NZ, stride=8), :] = south(2 + n) - x["fs"][n]
        gl_ref[pl.ds(2 * n + 1, NZ, stride=8), :] = north(2 + n) + x["gn"][n]
        b_scr[pl.ds(2 * n, NZ, stride=8), :] = south(4)
        b_scr[pl.ds(2 * n + 1, NZ, stride=8), :] = north(4)
    zero = jnp.zeros((NZ, 128), F32)
    for n in range(4, 8):
        gl_ref[pl.ds(n, NZ, stride=8), :] = zero
        b_scr[pl.ds(n, NZ, stride=8), :] = zero
    z8 = jnp.zeros((8, 128), F32)
    chains = [[z8, z8], [z8, z8]]
    for k, side in inward(NZ):
        here, here8 = pl.ds(k * NY, NY), pl.ds(k * 8, 8)
        b = b_scr[pl.ds((k - side) * 8, 8), :]
        behind, g = chains[side]
        r = 1.0 / (1.0 + behind + b - behind * g)
        g = b * r
        chains[side][:] = b, g
        gr_ref[here8, :] = r
        gg_ref[here8, :] = g
        lt_ref[here, :] = lt_in[here, :]
        ls_ref[here, :] = ls_in[here, :]
        pe, qe = pe_ref[here, :], qe_ref[here, :]
        pn, qn = pn_ref[pl.ds(k * NY + 8, NY), :], qn_ref[pl.ds(k * NY + 8, NY), :]
        ps, qs = pn_ref[pl.ds(k * NY + 7, NY), :], qn_ref[pl.ds(k * NY + 7, NY), :]
        a0_ref[here, :] = 1.0 - (pe - roll(qe, 1)) - (pn - qs)
        ae_ref[here, :] = -qe
        aw_ref[here, :] = roll(pe, 1)
        an_ref[here, :] = -qn
        as_ref[here, :] = ps
    for n, ref in enumerate((lt_ref, ls_ref)):
        ref[low, :] = ref[low, :] + x["fs"][n]
        ref[top, :] = ref[top, :] - x["fn"][n]
    a0_ref[low, :] = a0_ref[low, :] + x["bes"]
    a0_ref[top, :] = a0_ref[top, :] - x["p15"]
    as_ref[low, :] = x["als"]
    an_ref[top, :] = -x["q15"]


def steps_kernel(NZ, NY, last, pos_ref, ra_ref, rb_ref, own_ref, lt_ref, ls_ref, a0_ref, ae_ref, aw_ref, an_ref, as_ref,
                 r_ref, g_ref, gl_ref, gr_ref, gg_ref, bot_ref, to_ref, so_ref,
                 yt, ys, ct, cs, yte, yse, re_s, ge_s, yr, xt, xs, sems):
    shape = (NY, 128)
    PAD = NY + 16
    lane = lane_of(shape)
    lane8 = lane_of((8, 128))
    edge = (lane == 0) | (lane == 127)
    edge8 = (lane8 == 0) | (lane8 == 127)
    even, even8 = lax.rem(lane, 2) == 0, lax.rem(lane8, 2) == 0
    klane = lax.shift_right_logical(lane, 1).astype(F32)
    klane8 = lax.shift_right_logical(lane8, 1).astype(F32)

    odd_lon = lax.rem(lax.div(pos_ref[0], last + 1), 2) == 1
    base = 4 * NY

    def own(start, size):
        return own_ref[start : start + size, :]

    def received(start, size):
        a, b = ra_ref[start : start + size, :], rb_ref[start : start + size, :]
        return jnp.where(odd_lon, a, b), jnp.where(odd_lon, b, a)

    def spread(x, col, size):
        return jnp.broadcast_to(x[:, col : col + 1], (size, 128))

    ghosts = []
    for n in range(4):
        west, east = received(n * NY, NY)
        if n == 0:
            bg_east, bg_west = spread(east, 96, NY), spread(west, 96, NY)
        ghosts.append(jnp.where(even, east, roll(west, 1)))
        ghosts.append(jnp.where(even, roll(east, -1), west))
    west, east = received(base, 8)
    bg8 = jnp.where(even8, spread(east, 96, 8), spread(west, 96, 8))
    corners = jnp.where(even8, roll(east, -1), roll(west, 1))
    bot = bot_ref[...]
    botf = bot.astype(F32)
    bo = jnp.where(even, spread(botf, 127, NY), spread(botf, 0, NY))
    bg = jnp.where(even, bg_east, bg_west)
    wo, wg = (klane < bo).astype(F32), (klane < bg).astype(F32)
    bot_edge = jnp.where(lane == 127, bg_east, bg_west)
    po = jnp.where(even, own(2 * NY, NY), 0.0)
    qo = jnp.where(even, own(3 * NY, NY), 0.0)
    pg = jnp.where(even, 0.0, ghosts[6])
    qg = jnp.where(even, 0.0, ghosts[7])
    alpha = wo * pg - wg * qo
    beta = wo * qg - wg * po
    corr = [alpha * ghosts[n] + beta * own(n * NY, NY) for n in range(2)]
    glat = [ghosts[2 + n] - corr[n] for n in range(2)]
    gr, gg = ghosts[4], ghosts[5]

    bot_rows = own(base + 24, 8)
    bo8 = jnp.where(even8, spread(bot_rows, 127, 8), spread(bot_rows, 0, 8))
    wo8, wg8 = (klane8 < bo8).astype(F32), (klane8 < bg8).astype(F32)
    first_two = row_of((8, 128)) < 2
    pg8 = jnp.where(first_two, roll(corners, -4, 0), roll(corners, -2, 0))
    qg8 = jnp.where(first_two, roll(corners, -6, 0), roll(corners, -4, 0))
    co, po8, qo8 = own(base, 8), own(base + 8, 8), own(base + 16, 8)
    corner = wo8 * (pg8 * corners + qg8 * co) - wg8 * (po8 * co + qo8 * corners)

    z, z8 = jnp.zeros(shape, F32), jnp.zeros((8, 128), F32)
    state = [(z, z, z, z, z, z, z8, z8)] * 2
    last_r = [None, None]
    for k, side in inward(NZ):
        y0, y1, e0, e1, gp, gep, yrow, ggp = state[side]
        here, here8 = pl.ds(k * NY, NY), pl.ds(k * 8, 8)
        turn = 127 - 2 * k
        y0 = lt_ref[here, :] + jnp.where(edge, roll(corr[0], turn), 0.0) + gp * y0
        y1 = ls_ref[here, :] + jnp.where(edge, roll(corr[1], turn), 0.0) + gp * y1
        e0 = roll(glat[0], turn) + gep * e0
        e1 = roll(glat[1], turn) + gep * e1
        yrow = gl_ref[here8, :] + jnp.where(edge8, roll(corner, turn), 0.0) + ggp * yrow
        yt[here, :] = y0
        ys[here, :] = y1
        yte[here, :] = e0
        yse[here, :] = e1
        yr[here8, :] = yrow
        gep = roll(gg, turn)
        rep = roll(gr, turn)
        re_s[here, :] = rep
        ge_s[here, :] = gep
        gp, ggp = g_ref[here, :], gg_ref[here8, :]
        state[side] = y0, y1, e0, e1, gp, gep, yrow, ggp
        if abs(2 * k + 1 - NZ) == 1:
            last_r[side] = r_ref[here, :], rep, gr_ref[here8, :]

    found = []
    for y, r, g in ((0, 0, 4), (1, 0, 4), (2, 1, 5), (3, 1, 5), (6, 2, 7)):
        found.append(meet(*[(last_r[side][r], state[side][g], state[side][y]) for side in range(2)]))
    state = [tuple(x[side] for x in found) for side in range(2)]
    for k, side in reversed(inward(NZ)):
        x0, x1, e0, e1, xr = state[side]
        here, here8 = pl.ds(k * NY, NY), pl.ds(k * 8, 8)
        inner = pl.ds(k * PAD + 8, NY)
        r, g = r_ref[here, :], g_ref[here, :]
        x0 = r * yt[here, :] + g * x0
        x1 = r * ys[here, :] + g * x1
        w = k < bot
        ct[inner, :] = jnp.where(w, x0, 0.0)
        cs[inner, :] = jnp.where(w, x1, 0.0)
        r, g = re_s[here, :], ge_s[here, :]
        e0 = r * yte[here, :] + g * e0
        e1 = r * yse[here, :] + g * e1
        we = k < bot_edge
        yte[here, :] = jnp.where(we, e0, 0.0)
        yse[here, :] = jnp.where(we, e1, 0.0)
        xr = gr_ref[here8, :] * yr[here8, :] + gg_ref[here8, :] * xr
        state[side] = x0, x1, e0, e1, xr
        c = jnp.where(k < bot_rows, xr, 0.0)
        ct[pl.ds(k * PAD + 7, 1), :] = c[0:1, :]
        ct[pl.ds(k * PAD + 8 + NY, 1), :] = c[1:2, :]
        cs[pl.ds(k * PAD + 7, 1), :] = c[2:3, :]
        cs[pl.ds(k * PAD + 8 + NY, 1), :] = c[3:4, :]

    state = [(z, z, z)] * 2
    for k, side in inward(NZ):
        y0, y1, gp = state[side]
        here = pl.ds(k * NY, NY)
        turn = 127 - 2 * k
        al = roll(alpha, turn)
        a0 = a0_ref[here, :] + jnp.where(edge, roll(beta, turn), 0.0)
        ae = jnp.where(lane == 127, al, ae_ref[here, :])
        aw = jnp.where(lane == 0, al, aw_ref[here, :])
        an, as_ = an_ref[here, :], as_ref[here, :]
        ys_new = []
        for c_ref, e_ref in ((ct, yte), (cs, yse)):
            c = c_ref[pl.ds(k * PAD + 8, NY), :]
            rim = e_ref[here, :]
            east = jnp.where(lane == 127, rim, roll(c, -1))
            west = jnp.where(lane == 0, rim, roll(c, 1))
            ys_new.append(
                a0 * c + (ae * east + aw * west)
                + (an * c_ref[pl.ds(k * PAD + 9, NY), :] + as_ * c_ref[pl.ds(k * PAD + 7, NY), :])
            )
        y0 = ys_new[0] + gp * y0
        y1 = ys_new[1] + gp * y1
        yt[here, :] = y0
        ys[here, :] = y1
        state[side] = y0, y1, g_ref[here, :]

    middle = [pl.ds((NZ // 2 - 1 + side) * NY, NY) for side in range(2)]
    found = [meet(*[(r_ref[middle[side], :], state[side][2], state[side][n]) for side in range(2)]) for n in range(2)]
    state = [tuple(x[side] for x in found) for side in range(2)]
    part = max(NZ // CHUNKS, 1)
    copies = []
    for k, side in reversed(inward(NZ)):
        x0, x1 = state[side]
        here = pl.ds(k * NY, NY)
        r, g = r_ref[here, :], g_ref[here, :]
        x0 = r * yt[here, :] + g * x0
        x1 = r * ys[here, :] + g * x1
        w = k < bot
        xt[here, :] = jnp.where(w, x0, 0.0)
        xs[here, :] = jnp.where(w, x1, 0.0)
        state[side] = x0, x1
        if (k + side) % part == 0:
            chunk = pl.ds((k // part) * part * NY, part * NY)
            for n, (src, dst) in enumerate(((xt, to_ref), (xs, so_ref))):
                copy = pltpu.make_async_copy(src.at[chunk], dst.at[chunk], sems.at[n, k // part])
                copy.start()
                copies.append(copy)
    for copy in copies:
        copy.wait()


VM = pl.BlockSpec(memory_space=pltpu.VMEM)
SM = pl.BlockSpec(memory_space=pltpu.SMEM)
HB = pl.BlockSpec(memory_space=pltpu.HBM)
CHUNKS = 4


def vmem(*shape):
    return pltpu.VMEM(shape, F32)


def call(kernel, ins, outs, out_specs=None, scratch=(), cost=0):
    return pl.pallas_call(
        kernel,
        out_shape=outs,
        in_specs=ins,
        out_specs=out_specs or [VM] * len(outs),
        scratch_shapes=list(scratch),
        compiler_params=pltpu.CompilerParams(vmem_limit_bytes=40 << 20),
        cost_estimate=pl.CostEstimate(flops=cost, bytes_accessed=cost, transcendentals=0) if cost else None,
    )


def per_device(temp, salt, east_speed, north_speed, mixing_h, mixing_v, wet, bottom):
    NZ, NY, NX = temp.shape
    count_lat, count_lon = lax.axis_size("lat"), lax.axis_size("lon")
    last = count_lat - 1
    size = NZ * NY
    flat = vmem(size, NX)
    fields = (temp, salt, east_speed, north_speed, mixing_h, mixing_v)
    axes = ("lon", "lat")
    pos = lax.axis_index(axes).astype(jnp.int32).reshape(1)
    first, second = lat_routes(count_lon, count_lat)

    msg_a, msg_a2, msg_b, tails = call(
        functools.partial(rows_kernel, NZ, NY, last),
        [SM] + [HB] * 7,
        [vmem(NFIRST * NZ + 8, NX), vmem((NF - NFIRST) * NZ, NX), vmem(NF * NZ + 8, NX), vmem(16, NX)],
        scratch=[vmem(NZ, NY, NX)] * 6 + [pltpu.VMEM((NY, NX), jnp.int32), pltpu.SemaphoreType.DMA((7, 2))],
    )(pos, *[pltpu.with_memory_space_constraint(a, pltpu.HBM) for a in fields], pltpu.with_memory_space_constraint(bottom, pltpu.HBM))
    t, s, u, v, h, m = (a.reshape(size, NX) for a in fields)
    bot = bottom
    ra = lax.ppermute(msg_a, axes, first)
    rb = lax.ppermute(msg_b, axes, second)
    upward = [(x, y) for x, y in first if NFIRST < 5 or x % count_lat % 2]
    ra2 = lax.ppermute(msg_a2, axes, upward)
    lt, ls, pe, qe, pn, qn, r, g, pk = call(
        functools.partial(block_kernel, NZ, NY), [VM] * 7,
        [flat] * 4 + [vmem(size + 8, NX)] * 2 + [flat] * 2 + [vmem(8 * NY, NX)], cost=10_000_000,
    )(t, s, u, v, h, m, bot)
    col_msg = vmem(4 * NY + 8, NX)
    cols_a, cols_b, own = call(
        functools.partial(columns_kernel, NZ, NY, last), [SM] + [VM] * 5, [col_msg] * 2 + [vmem(4 * NY + 32, NX)]
    )(pos, ra, rb, tails, bot, pk)
    ca = lax.ppermute(cols_a, "lon", [(i, i ^ 1) for i in range(count_lon)])
    cb = lax.ppermute(cols_b, "lon", [(i, (i + 1 if i % 2 else i - 1) % count_lon) for i in range(count_lon)])
    ghost = vmem(NZ * 8, NX)
    lt, ls, a0, ae, aw, an, as_, gl, gr, gg = call(
        functools.partial(ghost_rows_kernel, NZ, NY, last), [SM] + [VM] * 14, [flat] * 7 + [ghost] * 3,
        scratch=[ghost], cost=10_000_000,
    )(pos, ra, ra2, rb, t, s, v, h, bot, lt, ls, pe, qe, pn, qn)
    pad = vmem(NZ * (NY + 16), NX)
    out = call(
        functools.partial(steps_kernel, NZ, NY, last), [SM] + [VM] * 16,
        [jax.ShapeDtypeStruct((size, NX), F32)] * 2, out_specs=[HB] * 2,
        scratch=[flat] * 2 + [pad] * 2 + [flat] * 4 + [ghost] + [flat] * 2 + [pltpu.SemaphoreType.DMA((2, CHUNKS))],
    )(pos, ca, cb, own, lt, ls, a0, ae, aw, an, as_, r, g, gl, gr, gg, bot)
    return tuple(o.reshape(temp.shape) for o in out)


def solution(mesh):
    field = P(None, "lat", "lon")
    return jax.shard_map(
        per_device,
        mesh=mesh,
        in_specs=(field,) * 7 + (P("lat", "lon"),),
        out_specs=(field, field),
        check_vma=False,
    )
```
